512 devices in a mesh: row: 64 (over x, z), col: 8 (over y, core).
Axes of the slice: x: 4, y: 4, z: 16, core: 2. Of those that a mesh axis runs over, the one named last changes fastest.
Arguments:
- kelvin_start: float32 [512, 512, 128], P('row', 'col'), may hold values from 1 to 2.5
- mass_ratio: float32 [512, 512, 128], P('row', 'col'), may hold values from 0.6 to 1
- material_region_labels: int32 [512, 512], P('row', 'col'), may hold values from 0 to 7
- pristine_conductivity: float32 [8], replicated, may hold values from 0.5 to 2
- burnt_conductivity: float32 [8], replicated, may hold values from 0.5 to 2
- burnt_mass_ratio: float32 [8], replicated, may hold values from 0.25 to 0.5
- arrhenius_prefactor: float32 [8], replicated, may hold values from 1 to 30
- onset_kelvin: float32 [8], replicated, may hold values from 2 to 6
- exchange_film_strength: float32 [64, 8, 64, 128], P('row', 'col'), may hold values from 0.25 to 4
- stagnation_kelvin: float32 [64, 8, 64, 128], P('row', 'col'), may hold values from 2 to 6
- receiving_element: int32 [64, 8, 64, 128], P('row', 'col'), may hold values from 0 to 511
- occupied_slot_totals: int32 [64, 8, 64], P('row', 'col'), may hold values from 16 to 128, as said below
Outputs:
- kelvin_after: float32 [512, 512, 128], P('row', 'col')
- mass_ratio_after: float32 [512, 512, 128], P('row', 'col')
The draws below stay inside these ranges and needn't reach their ends.
Inputs may be any that keep to these rules, and one draw needn't show every extreme that they name: `occupied_slot_totals`: live slots come first in each block; in every col one destination tile receives 128 live faces from every source; slots at or past the count hold arbitrary values. `receiving_element`: cell i * 64 + j is row i and column j of the destination tile.
All inputs are finite; a program needn't handle non-finite values.
Results may differ from the reference program's by a relative error of at most 0.0003.
Values sent between devices are 32-bit elements; how exact they have to be, the bound alone decides.
A program may use at most 64 MiB of HBM per device.

```python
import math
import jax
import jax.numpy as jnp
from jax import lax

CX = 8
CY = 64
LAYER_TOTAL = 128
ZONES = 8
SLOT_LIMIT = 128
R_X = 32
R_Y = 64
SPAN_LEADING = 512
SPAN_TRAILING = 512
R_Z = 1024
EXTERIOR_SHARE = 16
N_ROW = 64
N_COL = 8


def draw_occupied_slot_totals(key, part):
    light_key, heavy_key, pick_key = jax.random.split(key, 3)
    light_load = jax.random.randint(light_key, (N_ROW, N_COL, N_ROW), SLOT_LIMIT // 8, SLOT_LIMIT // 4 + 1)
    heavy_load = jax.random.randint(heavy_key, (N_ROW, N_COL, N_ROW), SLOT_LIMIT // 2, SLOT_LIMIT + 1)

    def one_order(subkey):
        return jax.random.permutation(subkey, N_ROW)
    tile_rank = jax.vmap(one_order)(jax.random.split(pick_key, N_COL))
    busy_tile = tile_rank < max(1, N_ROW // 5)
    full_tile = tile_rank == 0
    counts = jnp.where(busy_tile[None], heavy_load, light_load)
    counts = jnp.where(full_tile[None], SLOT_LIMIT, counts)
    return counts.astype(jnp.int32)


def draw_kelvin_start(key, part):
    key = jax.random.fold_in(key, 11)
    phase_key, noise_key = jax.random.split(key)
    phase = jax.random.randint(phase_key, (), 0, 2)
    lead = jnp.arange(SPAN_LEADING, dtype=jnp.int32)[:, None, None]
    trail = jnp.arange(SPAN_TRAILING, dtype=jnp.int32)[None, :, None]
    noise = jax.random.uniform(noise_key, (SPAN_LEADING, SPAN_TRAILING, LAYER_TOTAL), jnp.float32)
    width_lead = 4 * CX
    width_trail = max(CY // 2, 1)
    plateau = ((lead // width_lead + trail // width_trail + phase) % 2).astype(jnp.float32)
    value = 0.55 * plateau + 0.45 * noise
    return (1.0 + 1.5 * value).astype(jnp.float32)


def with_ends(array, own_key, low, top_value):
    shape = array.shape
    place = [jax.random.randint(jax.random.fold_in(own_key, axis), (), 0, shape[axis]) for axis in range(len(shape))]
    array = array.at[tuple(place)].set(low)
    longest = shape.index(max(shape))
    place[longest] = (place[longest] + 1) % shape[longest]
    return array.at[tuple(place)].set(top_value)


def block_scale(stream_key, shape, cuts, low, top_value):
    def one(position, parts):
        heights = jax.random.uniform(jax.random.fold_in(jax.random.fold_in(stream_key, 6), position), (parts,), jnp.float32, low / len(cuts), top_value / len(cuts))
        return jnp.repeat(jnp.exp(heights), shape[position] // parts).reshape((-1,) + (1,) * (len(shape) - position - 1))

    level = one(*cuts[0])
    for cut in cuts[1:]:
        level = level * one(*cut)
    return level


def setup_inputs(seed: int = 0) -> dict:
    key_of = jax.random.split(jax.random.key(seed), 13)
    kelvin_start = draw_kelvin_start(jax.random.fold_in(key_of[12], 71), 0)
    mass_ratio = jnp.clip(0.6 + 0.39999998 * jax.random.uniform(key_of[1], (SPAN_LEADING, SPAN_TRAILING, LAYER_TOTAL), jnp.float32) ** block_scale(key_of[1], (SPAN_LEADING, SPAN_TRAILING, LAYER_TOTAL), ((0, 64), (1, 8)), -0.2, 0.2), 0.6, 1.0)
    material_region_labels = with_ends(jax.random.randint(key_of[2], (SPAN_LEADING, SPAN_TRAILING), 0, ZONES), jax.random.fold_in(key_of[2], 1), 0, ZONES - 1).astype(jnp.int32)
    pristine_conductivity = jnp.clip(jnp.exp(jax.random.uniform(key_of[3], (ZONES,), jnp.float32, math.log(0.5), math.log(2.0))), 0.5, 2.0)
    burnt_conductivity = jnp.clip(jnp.exp(jax.random.uniform(key_of[4], (ZONES,), jnp.float32, math.log(0.5), math.log(2.0))), 0.5, 2.0)
    burnt_mass_ratio = jnp.clip(jax.random.uniform(key_of[5], (ZONES,), jnp.float32, 0.25, 0.5), 0.25, 0.5)
    arrhenius_prefactor = jnp.clip(jnp.exp(jax.random.uniform(key_of[6], (ZONES,), jnp.float32, math.log(1.0), math.log(30.0))), 1.0, 30.0)
    onset_kelvin = jnp.clip(jax.random.uniform(key_of[7], (ZONES,), jnp.float32, 2.0, 6.0), 2.0, 6.0)
    exchange_film_strength = jnp.clip(jnp.exp(math.log(4.0) - 2.7725887 * jax.random.uniform(key_of[8], (N_ROW, N_COL, N_ROW, SLOT_LIMIT), jnp.float32) ** block_scale(key_of[8], (N_ROW, N_COL, N_ROW, SLOT_LIMIT), ((0, 64), (1, 8)), -0.2, 0.2)), 0.25, 4.0)
    stagnation_kelvin = jnp.clip(2.0 + 4.0 * jax.random.uniform(key_of[9], (N_ROW, N_COL, N_ROW, SLOT_LIMIT), jnp.float32) ** block_scale(key_of[9], (N_ROW, N_COL, N_ROW, SLOT_LIMIT), ((0, 64), (1, 8)), -0.2, 0.2), 2.0, 6.0)
    receiving_element = with_ends(jax.random.randint(key_of[10], (N_ROW, N_COL, N_ROW, SLOT_LIMIT), 0, CX * CY), jax.random.fold_in(key_of[10], 1), 0, (CX * CY) - 1).astype(jnp.int32)
    occupied_slot_totals = draw_occupied_slot_totals(jax.random.fold_in(key_of[12], 71), 0)
    return {"kelvin_start": kelvin_start, "mass_ratio": mass_ratio, "material_region_labels": material_region_labels, "pristine_conductivity": pristine_conductivity, "burnt_conductivity": burnt_conductivity, "burnt_mass_ratio": burnt_mass_ratio, "arrhenius_prefactor": arrhenius_prefactor, "onset_kelvin": onset_kelvin, "exchange_film_strength": exchange_film_strength, "stagnation_kelvin": stagnation_kelvin, "receiving_element": receiving_element, "occupied_slot_totals": occupied_slot_totals}


HEAT_OF_PYROLYSIS = 0.3


def take_part(values, first_index, end_index, stride, solve_dim):
    return lax.slice_in_dim(values, first_index, end_index, stride, solve_dim)


def extend_end(values, filler, solve_dim):
    new_shape = list(values.shape)
    new_shape[solve_dim] = 1
    return jnp.concatenate([values, jnp.full(new_shape, filler, values.dtype)], solve_dim)


def merge_halves(even_value, odd_value, odd_count, solve_dim):
    even_head = take_part(even_value, 0, odd_count, 1, solve_dim)
    paired = jnp.stack([even_head, odd_value], solve_dim + 1)
    new_shape = list(even_head.shape)
    new_shape[solve_dim] = 2 * odd_count
    merged = paired.reshape(new_shape)
    if even_value.shape[solve_dim] > odd_count:
        merged = jnp.concatenate([merged, take_part(even_value, odd_count, odd_count + 1, 1, solve_dim)], solve_dim)
    return merged


def cyclic_solve(sub_diag, main_diag, super_diag, rights, solve_dim):
    length = main_diag.shape[solve_dim]
    if length == 1:
        return [vector / main_diag for vector in rights]
    odd_count = length // 2
    even_count = length - odd_count
    even_parts = [take_part(operand, 0, length, 2, solve_dim) for operand in (sub_diag, main_diag, super_diag)]
    odd_parts = [take_part(operand, 1, length, 2, solve_dim) for operand in (sub_diag, main_diag, super_diag)]
    even_rights = [take_part(vector, 0, length, 2, solve_dim) for vector in rights]
    odd_rights = [take_part(vector, 1, length, 2, solve_dim) for vector in rights]
    left_sub, left_main, left_super = [take_part(operand, 0, odd_count, 1, solve_dim) for operand in even_parts]
    left_rights = [take_part(vector, 0, odd_count, 1, solve_dim) for vector in even_rights]
    right_sub = take_part(extend_end(even_parts[0], 0.0, solve_dim), 1, odd_count + 1, 1, solve_dim)
    right_main = take_part(extend_end(even_parts[1], 1.0, solve_dim), 1, odd_count + 1, 1, solve_dim)
    right_super = take_part(extend_end(even_parts[2], 0.0, solve_dim), 1, odd_count + 1, 1, solve_dim)
    right_rights = [take_part(extend_end(vector, 0.0, solve_dim), 1, odd_count + 1, 1, solve_dim) for vector in even_rights]
    left_factor = -odd_parts[0] / left_main
    right_factor = -odd_parts[2] / right_main
    reduced_sub = left_factor * left_sub
    reduced_main = odd_parts[1] + left_factor * left_super + right_factor * right_sub
    reduced_super = right_factor * right_super
    reduced_rights = [odd_part + left_factor * left_part + right_factor * right_part
                      for odd_part, left_part, right_part in zip(odd_rights, left_rights, right_rights)]
    odd_solutions = cyclic_solve(reduced_sub, reduced_main, reduced_super, reduced_rights, solve_dim)
    results = []
    for even_part, odd_part in zip(even_rights, odd_solutions):
        edge_shape = list(odd_part.shape)
        edge_shape[solve_dim] = 1
        zero_plane = jnp.zeros(edge_shape, odd_part.dtype)
        padded = jnp.concatenate([zero_plane, odd_part, zero_plane], solve_dim)
        before = take_part(padded, 0, even_count, 1, solve_dim)
        after_vals = take_part(padded, 1, even_count + 1, 1, solve_dim)
        even_value = (even_part - even_parts[0] * before - even_parts[2] * after_vals) / even_parts[1]
        results.append(merge_halves(even_value, odd_part, odd_count, solve_dim))
    return results


def sweep_coefficients(capacity, diffuse_thermal_energy, diffusion, solve_dim):
    length = diffuse_thermal_energy.shape[solve_dim]
    face_cond = 0.5 * (take_part(diffuse_thermal_energy, 0, length - 1, 1, solve_dim) + take_part(diffuse_thermal_energy, 1, length, 1, solve_dim))
    edge_shape = list(diffuse_thermal_energy.shape)
    edge_shape[solve_dim] = 1
    zero_edge = jnp.zeros(edge_shape, diffuse_thermal_energy.dtype)
    sub_diag = -diffusion * jnp.concatenate([zero_edge, face_cond], solve_dim)
    super_diag = -diffusion * jnp.concatenate([face_cond, zero_edge], solve_dim)
    main_diag = capacity - sub_diag - super_diag
    return sub_diag, main_diag, super_diag


def solve_lines(pieces, diffusion, solve_dim):
    sub_diag, main_diag, super_diag = sweep_coefficients(pieces[1], pieces[2], diffusion, solve_dim)
    return cyclic_solve(sub_diag, main_diag, super_diag, [pieces[0]], solve_dim)[0]


def column_values(material_region_labels, property_arrays):
    matches = (material_region_labels[..., None] == jnp.arange(property_arrays[0].shape[0], dtype=jnp.int32)).astype(jnp.float32)
    return [jnp.sum(matches * lookup, axis=-1)[..., None] for lookup in property_arrays]


def decompose_through_layers(kelvin_start, mass_ratio, material_region_labels, property_arrays, exterior_multiplier, exterior_flux_amount):
    virgin, charred, residue, rate_col, energy = column_values(material_region_labels, property_arrays)
    old_conduct = charred + (virgin - charred) * (mass_ratio - residue) / (1.0 - residue)
    thickness_dimension = kelvin_start.ndim - 1
    sub_diag, main_diag, super_diag = sweep_coefficients(mass_ratio, old_conduct, float(R_Z), thickness_dimension)
    main_diag = main_diag.at[..., 0].add(float(EXTERIOR_SHARE) * exterior_multiplier)
    forcing_vector = (mass_ratio * kelvin_start).at[..., 0].add(float(EXTERIOR_SHARE) * exterior_flux_amount)
    depth_temp = cyclic_solve(sub_diag, main_diag, super_diag, [forcing_vector], thickness_dimension)[0]
    extent = rate_col * jnp.exp(-energy / depth_temp)
    mass_ratio_after = residue + (mass_ratio - residue) * jnp.exp(-extent)
    warmed_fields = depth_temp - HEAT_OF_PYROLYSIS * (mass_ratio - mass_ratio_after) / mass_ratio_after
    diffuse_thermal_energy = charred + (virgin - charred) * (mass_ratio_after - residue) / (1.0 - residue)
    return warmed_fields, mass_ratio_after, diffuse_thermal_energy


def reference(kelvin_start, mass_ratio, material_region_labels, pristine_conductivity, burnt_conductivity, burnt_mass_ratio, arrhenius_prefactor, onset_kelvin, exchange_film_strength, stagnation_kelvin, receiving_element, occupied_slot_totals):
    slot_index = jnp.arange(SLOT_LIMIT, dtype=jnp.int32)
    live_slots = (slot_index < occupied_slot_totals[..., None]).astype(jnp.float32)
    blending_shares = exchange_film_strength * live_slots
    flux_arriving = blending_shares * stagnation_kelvin
    tile_rows = jnp.arange(N_ROW, dtype=jnp.int32)[None, None, :, None]
    tile_cols = jnp.arange(N_COL, dtype=jnp.int32)[None, :, None, None]
    global_x = tile_rows * CX + receiving_element // CY
    global_y = tile_cols * CY + receiving_element % CY
    flat_ids = (global_x * SPAN_TRAILING + global_y).reshape(-1).astype(jnp.int32)
    exterior_multiplier = jax.ops.segment_sum(blending_shares.reshape(-1), flat_ids, num_segments=SPAN_LEADING * SPAN_TRAILING).reshape(SPAN_LEADING, SPAN_TRAILING)
    exterior_flux_amount = jax.ops.segment_sum(flux_arriving.reshape(-1), flat_ids, num_segments=SPAN_LEADING * SPAN_TRAILING).reshape(SPAN_LEADING, SPAN_TRAILING)
    property_arrays = (pristine_conductivity, burnt_conductivity, burnt_mass_ratio, arrhenius_prefactor, onset_kelvin)

    def line_refresh(pieces):
        return decompose_through_layers(pieces[0], pieces[1], pieces[2], property_arrays, pieces[3], pieces[4])

    warmed_fields, mass_ratio_after, diffuse_thermal_energy = lax.map(line_refresh, (kelvin_start, mass_ratio, material_region_labels, exterior_multiplier, exterior_flux_amount))
    forcing_vector = mass_ratio_after * warmed_fields

    def solve_x(pieces):
        return solve_lines(pieces, float(R_X), 0)

    across = lax.map(solve_x, (jnp.swapaxes(forcing_vector, 0, 1), jnp.swapaxes(mass_ratio_after, 0, 1), jnp.swapaxes(diffuse_thermal_energy, 0, 1)))
    across = jnp.swapaxes(across, 0, 1)
    forcing_vector_other = mass_ratio_after * across

    def sweep_trailing_lines(pieces):
        return solve_lines(pieces, float(R_Y), 0)

    kelvin_after = lax.map(sweep_trailing_lines, (forcing_vector_other, mass_ratio_after, diffuse_thermal_energy))
    return kelvin_after, mass_ratio_after
```

```python
import functools

import jax
import jax.numpy as jnp
from jax import lax
from jax.experimental import pallas as pl
from jax.experimental.pallas import tpu as pltpu
from jax.sharding import PartitionSpec as P

R_X = 32.0
R_Y = 64.0
R_Z = 1024.0
EXTERIOR_SHARE = 16.0
HEAT_OF_PYROLYSIS = 0.3

MESH = pl.DeviceIdType.MESH
F32 = jnp.float32
BF16 = jnp.bfloat16

FACE_ROWS = 3
PORT_ROWS = 5
BACK_ROWS = 2
DEPTH_ROWS = 64


def kernel(
    n_row, n_col, cx, cy, depth,
    kel_h, mass_h, lab_h, virgin_h, charred_h, residue_h, rate_h, energy_h,
    film_h, stag_h, elem_h, count_h,
    out_h, mass_out_h,
    kel, mass, lab, virgin_s, charred_s, residue_s, rate_s, energy_s,
    film, stag, elem, count,
    props, sol_u, sol_v, first_u, first_v,
    face_s, face_r, split, cond, mass2, rhs,
    k_row_s, k_row_r, k_col_s, k_col_r,
    gx, lx, px, port_s, port_r, back_s, back_r,
    gy, dy, qy, ry, py, ypt_s, ypt_r, yrh_s, yrh_r, yfac, ysol, out,
    in_sem, out_sem, send_sem, recv_sem,
):
    row, col = lax.axis_index("row"), lax.axis_index("col")

    loads = [
        (film_h, film), (stag_h, stag), (elem_h, elem), (count_h, count),
        (kel_h, kel), (mass_h, mass), (lab_h, lab),
        (virgin_h, virgin_s), (charred_h, charred_s), (residue_h, residue_s),
        (rate_h, rate_s), (energy_h, energy_s),
    ]
    loads = [pltpu.make_async_copy(a, b, in_sem.at[i]) for i, (a, b) in enumerate(loads)]
    for load in loads:
        load.start()

    barrier = pltpu.get_barrier_semaphore()

    def greet_row(t, _):
        pl.semaphore_signal(
            barrier, inc=1, device_id={"row": lax.rem(row + t, n_row)}, device_id_type=MESH
        )
        return 0

    def greet_col(t, _):
        pl.semaphore_signal(
            barrier, inc=1, device_id={"col": lax.rem(col + t, n_col)}, device_id_type=MESH
        )
        return 0

    lax.fori_loop(1, n_row, greet_row, 0)
    lax.fori_loop(1, n_col, greet_col, 0)

    lane = lax.broadcasted_iota(jnp.int32, (cy, depth), 1)

    def strided(ref, value):
        return ref.at[pl.ds(value, ref.shape[0] // 8, stride=8), :]

    def slot(ref, index, rows):
        return ref.at[pl.ds(pl.multiple_of(index * 8, 8), rows), :]

    def exchange_row(source, target, rows, phase):
        def send(t, _):
            peer = lax.rem(row + t, n_row)
            pltpu.make_async_remote_copy(
                src_ref=slot(source, peer, rows),
                dst_ref=slot(target, row, rows),
                send_sem=send_sem.at[phase],
                recv_sem=recv_sem.at[phase],
                device_id={"row": peer},
                device_id_type=MESH,
            ).start()
            return 0

        lax.fori_loop(1, n_row, send, 0)
        slot(target, row, rows)[...] = slot(source, row, rows)[...]

    def row_bytes(ref, rows):
        return ref.at[pl.ds(0, (n_row - 1) * rows), :]

    def exchange_col(source, target, phase):
        def send(t, _):
            peer = lax.rem(col + t, n_col)
            pltpu.make_async_remote_copy(
                src_ref=source,
                dst_ref=target.at[col],
                send_sem=send_sem.at[phase],
                recv_sem=recv_sem.at[phase],
                device_id={"col": peer},
                device_id_type=MESH,
            ).start()
            return 0

        lax.fori_loop(1, n_col, send, 0)
        target[col] = source[...]

    def await_bytes(ref, sem):
        pltpu.make_async_copy(ref, ref, sem).wait()

    for load in loads[:4]:
        load.wait()
    counts = jnp.broadcast_to(count[...].astype(F32), (8, n_row)).T[:, 0:1]
    face_lane = lax.broadcasted_iota(jnp.int32, film.shape, 1).astype(F32)
    weight = jnp.where(face_lane < counts, film[...], 0.0)
    strided(face_s, 0)[...] = weight
    strided(face_s, 1)[...] = jnp.where(face_lane < counts, weight * stag[...], 0.0)
    strided(face_s, 2)[...] = elem[...].astype(F32)
    pl.semaphore_wait(barrier, n_row - 1 + n_col - 1)
    exchange_row(face_s, face_r, FACE_ROWS, 0)

    for load in loads[4:]:
        load.wait()
    zone = lab[...]

    def look_up(table):
        value = jnp.full(zone.shape, table[0], F32)
        for z in range(1, 8):
            value = jnp.where(zone == z, table[z], value)
        return value

    virgin, charred, residue = look_up(virgin_s), look_up(charred_s), look_up(residue_s)
    slope = (virgin - charred) / (1.0 - residue)
    table = jnp.concatenate(
        [charred, slope, residue, look_up(rate_s), look_up(energy_s)], axis=0
    ).T
    for p in range(5):
        for x in range(cx):
            props[p, x * cy : (x + 1) * cy, :] = jnp.broadcast_to(
                table[:, p * cx + x : p * cx + x + 1], (cy, depth)
            )

    def depth_sweep(x, _):
        rows = pl.ds(pl.multiple_of(x * cy, cy), cy)
        m = mass[rows, :]
        k = props[0, rows, :] + props[1, rows, :] * (m - props[2, rows, :])
        a = jnp.where(lane == 0, 0.0, (-0.5 * R_Z) * (pltpu.roll(k, 1, 1) + k))
        d = m - a - pltpu.roll(a, depth - 1, 1)
        b = m * kel[rows, :]
        e = jnp.where(lane == 0, 1.0, 0.0)
        step = 1
        while step < depth:
            inv = 1.0 / d
            h = a * inv
            back = depth - step
            al = a * pltpu.roll(inv, step, 1)
            d = d - al * a - pltpu.roll(a * h, back, 1)
            b = b - al * pltpu.roll(b, step, 1) - pltpu.roll(h * b, back, 1)
            e = e - al * pltpu.roll(e, step, 1) - pltpu.roll(h * e, back, 1)
            a = -al * pltpu.roll(a, step, 1)
            step *= 2
        inv = 1.0 / d
        u, v = b * inv, e * inv
        sol_u[rows, :] = u
        sol_v[rows, :] = v
        first_u[...] = jnp.where(lane == x, u[:, 0:1], first_u[...])
        first_v[...] = jnp.where(lane == x, v[:, 0:1], first_v[...])
        return 0

    first_u[...] = jnp.zeros(first_u.shape, F32)
    first_v[...] = jnp.zeros(first_v.shape, F32)
    lax.fori_loop(0, cx, depth_sweep, 0)

    await_bytes(row_bytes(face_r, FACE_ROWS), recv_sem.at[0])
    for j in range(2):
        value = strided(face_r, j)[...]
        high = value.astype(BF16).astype(F32)
        split[j] = high
        split[2 + j] = value - high
    place = strided(face_r, 2)[...]
    place_x = jnp.floor(place * (1.0 / cy))
    split[4] = place_x
    split[5] = place - place_x * cy
    slots = film.shape[1]
    x_index = lax.broadcasted_iota(jnp.int32, (cx, slots), 0).astype(F32)
    y_index = lax.broadcasted_iota(jnp.int32, (cy, slots), 0).astype(F32)

    def add_faces(pair, total):
        lefts, rights = [], []
        for half in range(2):
            src = pair * 2 + half
            in_x = x_index == split[4, pl.ds(src, 1), :]
            lefts.append(
                jnp.concatenate(
                    [jnp.where(in_x, split[j, pl.ds(src, 1), :], 0.0) for j in range(4)], axis=0
                )
            )
            rights.append(jnp.where(y_index == split[5, pl.ds(src, 1), :], 1.0, 0.0))
        left = jnp.concatenate(lefts, axis=1).astype(BF16)
        right = jnp.concatenate(rights, axis=1).astype(BF16)
        return total + lax.dot_general(
            right, left, (((1,), (1,)), ((), ())), preferred_element_type=F32
        )

    sums = lax.fori_loop(0, n_row // 2, add_faces, jnp.zeros((cy, 4 * cx), F32), unroll=True)
    wall_w = sums[:, 0:cx] + sums[:, 2 * cx : 3 * cx]
    wall_q = sums[:, cx : 2 * cx] + sums[:, 3 * cx : 4 * cx]
    alpha = (
        EXTERIOR_SHARE
        * (wall_q - wall_w * first_u[:, 0:cx])
        / (1.0 + EXTERIOR_SHARE * wall_w * first_v[:, 0:cx])
    )

    def send_k(source, target, axis, position, size, phase):
        copy = pltpu.make_async_remote_copy(
            src_ref=source,
            dst_ref=target,
            send_sem=send_sem.at[phase],
            recv_sem=recv_sem.at[phase],
            device_id={axis: lax.rem(position + size - 1, size)},
            device_id_type=MESH,
        )
        copy.start()
        return copy

    for x in range(cx):
        rows = pl.ds(x * cy, cy)
        m = mass[rows, :]
        res = props[2, rows, :]
        t = sol_u[rows, :] + alpha[:, x : x + 1] * sol_v[rows, :]
        extent = props[3, rows, :] * jnp.exp(-props[4, rows, :] / t)
        excess = (m - res) * jnp.exp(-extent)
        m2 = res + excess
        mass2[rows, :] = m2
        rhs[rows, :] = m2 * t - HEAT_OF_PYROLYSIS * (m - m2)
        cond[rows, :] = props[0, rows, :] + props[1, rows, :] * excess
        if x == 0:
            k_row_s[...] = cond[rows, :]
            k_row = send_k(k_row_s, k_row_r, "row", row, n_row, 1)
    mass_out = pltpu.make_async_copy(mass2, mass_out_h, out_sem.at[0])
    mass_out.start()
    k_col_s[...] = cond[pl.ds(0, cx, stride=cy), :]
    k_col = send_k(k_col_s, k_col_r, "col", col, n_col, 2)

    def plane(ref, x):
        return ref[pl.ds(x * cy, cy), :]

    face = (0.5 * R_X) * (plane(cond, 0) + plane(cond, 1))
    left = plane(mass2, 0) + face
    left_rhs = plane(rhs, 0)
    coupling, held, right_hand = face, face, plane(rhs, 1)
    for x in range(1, cx):
        if x < cx - 1:
            face = (0.5 * R_X) * (plane(cond, x) + plane(cond, x + 1))
        else:
            k_row.wait_recv()
            face = (0.5 * R_X) * (plane(cond, x) + k_row_r[...])
            face = jnp.where(row == n_row - 1, 0.0, face)
        inv = 1.0 / (plane(mass2, x) + held + face)
        g, l, p = face * inv, coupling * inv, right_hand * inv
        gx[x], lx[x], px[x] = g, l, p
        left = left - coupling * l
        left_rhs = left_rhs + coupling * p
        coupling = coupling * g
        held = face - face * g
        if x < cx - 1:
            right_hand = plane(rhs, x + 1) + right_hand * g
        else:
            right_hand = right_hand * g
    for j, value in enumerate((left, -coupling, held, left_rhs, right_hand)):
        strided(port_s, j)[...] = value
    exchange_row(port_s, port_r, PORT_ROWS, 3)

    k_col.wait_recv()

    def line(ref, y):
        return ref[pl.ds(y, cx, stride=cy), :]

    k_first = k_col_r[...]
    face0 = (0.5 * R_Y) * (line(cond, 0) + line(cond, 1))

    def port_y(y, carry):
        left, coupling, held, k_here = carry
        after = lax.rem(y + 1, cy)
        k_next = jnp.where(after == 0, k_first, line(cond, after))
        face = (0.5 * R_Y) * (k_here + k_next)
        face = jnp.where((after == 0) & (col == n_col - 1), 0.0, face)
        inv = 1.0 / (line(mass2, y) + held + face)
        g, l = face * inv, coupling * inv
        gy[y], dy[y], qy[y] = g, inv, l
        return left - coupling * l, coupling * g, face - face * g, k_next

    left, coupling, held, _ = lax.fori_loop(
        1, cy, port_y, (line(mass2, 0) + face0, face0, face0, line(cond, 1)), unroll=7
    )
    ypt_s[0], ypt_s[1], ypt_s[2] = left, -coupling, held
    exchange_col(ypt_s, ypt_r, 4)

    await_bytes(row_bytes(port_r, PORT_ROWS), recv_sem.at[3])
    down = strided(port_r, 1)[...]
    a = pltpu.roll(down, 1, 0)
    d = strided(port_r, 0)[...] + pltpu.roll(strided(port_r, 2)[...], 1, 0)
    b = strided(port_r, 3)[...] + pltpu.roll(strided(port_r, 4)[...], 1, 0)
    step = 1
    while step < n_row:
        inv = 1.0 / d
        h = a * inv
        back = n_row - step
        al = a * pltpu.roll(inv, step, 0)
        d = d - al * a - pltpu.roll(a * h, back, 0)
        b = b - al * pltpu.roll(b, step, 0) - pltpu.roll(h * b, back, 0)
        a = -al * pltpu.roll(a, step, 0)
        step *= 2
    first = b / d
    strided(back_s, 0)[...] = first
    strided(back_s, 1)[...] = pltpu.roll(first, n_row - 1, 0)
    exchange_row(back_s, back_r, BACK_ROWS, 5)

    def answer_y(i, carry):
        q, r = carry
        y = cy - 1 - i
        g = gy[y]
        q, r = qy[y] + g * q, g * r
        qy[y], ry[y] = q, r
        return q, r

    zero = jnp.zeros((cx, depth), F32)
    lax.fori_loop(0, cy - 1, answer_y, (zero, zero + 1.0), unroll=7)
    qy[0], ry[0] = zero + 1.0, zero

    await_bytes(ypt_r.at[pl.ds(0, n_col - 1)], recv_sem.at[4])
    diag = ypt_r[0, 0]
    for i in range(n_col):
        inv = 1.0 / diag
        yfac[0, i] = inv
        if i < n_col - 1:
            off = ypt_r[i, 1]
            yfac[1, i] = off * inv
            diag = ypt_r[i + 1, 0] + ypt_r[i, 2] - off * off * inv

    await_bytes(row_bytes(back_r, BACK_ROWS), recv_sem.at[5])
    x_first, x_next = strided(back_r, 0)[...], strided(back_r, 1)[...]
    rhs[pl.ds(0, cy), :] = x_first * plane(mass2, 0)
    for x in range(cx - 1, 0, -1):
        x_next = px[x] + gx[x] * x_next + lx[x] * x_first
        rhs[pl.ds(x * cy, cy), :] = x_next * plane(mass2, x)

    def gather_rhs(y, carry):
        value = line(rhs, y)
        return carry[0] + qy[y] * value, carry[1] + ry[y] * value

    total = lax.fori_loop(0, cy, gather_rhs, (zero, zero), unroll=8)
    yrh_s[0], yrh_s[1] = total
    exchange_col(yrh_s, yrh_r, 6)

    def forward_y(y, carry):
        carry = line(rhs, y) + gy[y - 1] * carry
        py[y] = carry
        return carry

    def backward_y(i, carry):
        y = cy - 1 - i
        carry = py[y] * dy[y] + gy[y] * carry
        py[y] = carry
        return carry

    gy[0] = zero
    lax.fori_loop(1, cy, forward_y, zero, unroll=7)
    lax.fori_loop(0, cy - 1, backward_y, zero, unroll=7)
    py[0] = zero

    await_bytes(yrh_r.at[pl.ds(0, n_col - 1)], recv_sem.at[6])
    value = yrh_r[0, 0]
    ysol[0] = value
    for i in range(1, n_col):
        value = yrh_r[i, 0] + yrh_r[i - 1, 1] - yfac[1, i - 1] * value
        ysol[i] = value
    value = value * yfac[0, n_col - 1]
    ysol[n_col - 1] = value
    ysol[n_col] = zero
    for i in range(n_col - 2, -1, -1):
        value = ysol[i] * yfac[0, i] - yfac[1, i] * value
        ysol[i] = value
    y_first, y_next = ysol[col], ysol[col + 1]

    def finish(y, _):
        out[pl.ds(y, cx, stride=cy), :] = py[y] + qy[y] * y_first + ry[y] * y_next
        return 0

    lax.fori_loop(0, cy, finish, 0, unroll=8)
    result = pltpu.make_async_copy(out, out_h, out_sem.at[1])
    result.start()

    await_bytes(row_bytes(face_s, FACE_ROWS), send_sem.at[0])
    k_row.wait_send()
    k_col.wait_send()
    await_bytes(row_bytes(port_s, PORT_ROWS), send_sem.at[3])
    await_bytes(ypt_r.at[pl.ds(0, n_col - 1)], send_sem.at[4])
    await_bytes(row_bytes(back_s, BACK_ROWS), send_sem.at[5])
    await_bytes(yrh_r.at[pl.ds(0, n_col - 1)], send_sem.at[6])
    mass_out.wait()
    result.wait()


def per_device(n_row, n_col, kelvin, mass, labels, virgin, charred, residue, rate, energy, film, stag, elem, count):
    cx, cy, depth = kelvin.shape
    slots = film.shape[-1]
    cells = cx * cy
    vmem = lambda *shape: pltpu.VMEM(shape, F32)
    zones = virgin.shape[0]
    scratch = [
        vmem(cells, depth), vmem(cells, depth), pltpu.VMEM((cx, cy), jnp.int32),
        *[pltpu.SMEM((zones,), F32)] * 5,
        vmem(n_row, slots), vmem(n_row, slots), pltpu.VMEM((n_row, slots), jnp.int32),
        pltpu.VMEM((1, n_row), jnp.int32),
        vmem(5, cells, depth), vmem(cells, depth), vmem(cells, depth), vmem(cy, depth), vmem(cy, depth),
        vmem(n_row * 8, slots), vmem(n_row * 8, slots), vmem(6, n_row, slots),
        vmem(cells, depth), vmem(cells, depth), vmem(cells, depth),
        vmem(cy, depth), vmem(cy, depth), vmem(cx, depth), vmem(cx, depth),
        vmem(cx, cy, depth), vmem(cx, cy, depth), vmem(cx, cy, depth),
        *[vmem(n_row * 8, depth)] * 4,
        *[vmem(cy, cx, depth)] * 5,
        vmem(3, cx, depth), vmem(n_col, 3, cx, depth),
        vmem(2, cx, depth), vmem(n_col, 2, cx, depth),
        vmem(2, n_col, cx, depth), vmem(n_col + 1, cx, depth), vmem(cells, depth),
        pltpu.SemaphoreType.DMA((12,)), pltpu.SemaphoreType.DMA((2,)),
        pltpu.SemaphoreType.DMA((7,)), pltpu.SemaphoreType.DMA((7,)),
    ]
    whole = jax.ShapeDtypeStruct((cells, depth), F32)
    out, mass_out = pl.pallas_call(
        functools.partial(kernel, n_row, n_col, cx, cy, depth),
        out_shape=(whole, whole),
        in_specs=[pl.BlockSpec(memory_space=pl.ANY)] * 12,
        out_specs=(pl.BlockSpec(memory_space=pl.ANY),) * 2,
        scratch_shapes=scratch,
        compiler_params=pltpu.CompilerParams(
            collective_id=0, has_side_effects=True, vmem_limit_bytes=24 * 1024 * 1024
        ),
    )(
        kelvin.reshape(cells, depth), mass.reshape(cells, depth), labels,
        virgin, charred, residue, rate, energy,
        film.reshape(n_row, slots), stag.reshape(n_row, slots), elem.reshape(n_row, slots),
        count.reshape(1, n_row),
    )
    return out.reshape(kelvin.shape), mass_out.reshape(kelvin.shape)


def solution(mesh):
    field, surface, faces = P("row", "col", None), P("row", "col"), P("row", "col", None, None)
    return jax.shard_map(
        functools.partial(per_device, mesh.shape["row"], mesh.shape["col"]),
        mesh=mesh,
        in_specs=(field, field, surface, P(), P(), P(), P(), P(), faces, faces, faces, field),
        out_specs=(field, field),
        check_vma=False,
    )
```

```python
import functools

import jax
import jax.numpy as jnp
from jax import lax
from jax.experimental import pallas as pl
from jax.experimental.pallas import tpu as pltpu
from jax.sharding import PartitionSpec as P

R_X = 32.0
R_Y = 64.0
R_Z = 1024.0
EXTERIOR_SHARE = 16.0
HEAT_OF_PYROLYSIS = 0.3

MESH = pl.DeviceIdType.MESH
F32 = jnp.float32
BF16 = jnp.bfloat16

N_X = 4
FACE_ROWS = 3
PORT_ROWS = 5
BACK_ROWS = 2


def kernel(
    n_row, n_col, cx, cy, depth,
    kel_h, mass_h, lab_h, virgin_h, charred_h, residue_h, rate_h, energy_h,
    film_h, stag_h, elem_h, count_h,
    out_h, mass_out_h,
    kel, mass, lab, virgin_s, charred_s, residue_s, rate_s, energy_s,
    film, stag, elem, count,
    props, sol_u, sol_v, first_u, first_v,
    face_s, face_r, split, cond, mass2, rhs,
    k_row_s, k_row_r, k_col_s, k_col_r,
    gx, lx, px, port_s, port_r, back_s, back_r,
    gy, dy, qy, ry, py, ypt_s, ypt_r, yrh_s, yrh_r, yfac, ysol, out,
    in_sem, out_sem, send_sem, recv_sem,
):
    row, col = lax.axis_index("row"), lax.axis_index("col")

    loads = [
        (film_h, film), (stag_h, stag), (elem_h, elem), (count_h, count),
        (kel_h, kel), (mass_h, mass), (lab_h, lab),
        (virgin_h, virgin_s), (charred_h, charred_s), (residue_h, residue_s),
        (rate_h, rate_s), (energy_h, energy_s),
    ]
    loads = [pltpu.make_async_copy(a, b, in_sem.at[i]) for i, (a, b) in enumerate(loads)]
    for load in loads:
        load.start()

    barrier = pltpu.get_barrier_semaphore()

    def far_first(n, size):
        return lax.rem(size + size // 2 + (n + 1) // 2 * (1 - 2 * lax.rem(n, 2)), size)

    n_z = n_row // N_X

    def row_peer(n):
        x = lax.rem(row // n_z + far_first(lax.rem(n, N_X), N_X), N_X)
        return x * n_z + lax.rem(lax.rem(row, n_z) + far_first(n // N_X, n_z), n_z)

    def greet_row(n, _):
        pl.semaphore_signal(barrier, inc=1, device_id={"row": row_peer(n)}, device_id_type=MESH)
        return 0

    def greet_col(t, _):
        pl.semaphore_signal(
            barrier, inc=1, device_id={"col": lax.rem(col + t, n_col)}, device_id_type=MESH
        )
        return 0

    lax.fori_loop(0, n_row - 1, greet_row, 0)
    lax.fori_loop(1, n_col, greet_col, 0)

    lane = lax.broadcasted_iota(jnp.int32, (cy, depth), 1)

    def strided(ref, value):
        return ref.at[pl.ds(value, ref.shape[0] // 8, stride=8), :]

    def slot(ref, index, rows):
        return ref.at[pl.ds(pl.multiple_of(index * 8, 8), rows), :]

    def exchange_row(source, target, rows, phase):
        def send(n, _):
            peer = row_peer(n)
            pltpu.make_async_remote_copy(
                src_ref=slot(source, peer, rows),
                dst_ref=slot(target, row, rows),
                send_sem=send_sem.at[phase],
                recv_sem=recv_sem.at[phase],
                device_id={"row": peer},
                device_id_type=MESH,
            ).start()
            return 0

        lax.fori_loop(0, n_row - 1, send, 0)
        slot(target, row, rows)[...] = slot(source, row, rows)[...]

    def row_bytes(ref, rows):
        return ref.at[pl.ds(0, (n_row - 1) * rows), :]

    def exchange_col(source, target, phase):
        def send(t, _):
            peer = lax.rem(col + t, n_col)
            pltpu.make_async_remote_copy(
                src_ref=source,
                dst_ref=target.at[col],
                send_sem=send_sem.at[phase],
                recv_sem=recv_sem.at[phase],
                device_id={"col": peer},
                device_id_type=MESH,
            ).start()
            return 0

        lax.fori_loop(1, n_col, send, 0)
        target[col] = source[...]

    def await_bytes(ref, sem):
        pltpu.make_async_copy(ref, ref, sem).wait()

    for load in loads[:4]:
        load.wait()
    counts = jnp.broadcast_to(count[...].astype(F32), (8, n_row)).T[:, 0:1]
    face_lane = lax.broadcasted_iota(jnp.int32, film.shape, 1).astype(F32)
    weight = jnp.where(face_lane < counts, film[...], 0.0)
    strided(face_s, 0)[...] = weight
    strided(face_s, 1)[...] = jnp.where(face_lane < counts, weight * stag[...], 0.0)
    strided(face_s, 2)[...] = elem[...].astype(F32)

    for load in loads[4:]:
        load.wait()
    zone = lab[...]

    def look_up(table):
        value = jnp.full(zone.shape, table[0], F32)
        for z in range(1, 8):
            value = jnp.where(zone == z, table[z], value)
        return value

    virgin, charred, residue = look_up(virgin_s), look_up(charred_s), look_up(residue_s)
    slope = (virgin - charred) / (1.0 - residue)
    table = jnp.concatenate(
        [charred, slope, residue, look_up(rate_s), look_up(energy_s)], axis=0
    ).T
    for p in range(5):
        for x in range(cx):
            props[p, x * cy : (x + 1) * cy, :] = jnp.broadcast_to(
                table[:, p * cx + x : p * cx + x + 1], (cy, depth)
            )

    def depth_sweep(x, _):
        rows = pl.ds(pl.multiple_of(x * cy, cy), cy)
        m = mass[rows, :]
        k = props[0, rows, :] + props[1, rows, :] * (m - props[2, rows, :])
        a = jnp.where(lane == 0, 0.0, (-0.5 * R_Z) * (pltpu.roll(k, 1, 1) + k))
        d = m - a - pltpu.roll(a, depth - 1, 1)
        b = m * kel[rows, :]
        e = jnp.where(lane == 0, 1.0, 0.0)
        step = 1
        while step < depth:
            inv = 1.0 / d
            h = a * inv
            back = depth - step
            al = a * pltpu.roll(inv, step, 1)
            d = d - al * a - pltpu.roll(a * h, back, 1)
            b = b - al * pltpu.roll(b, step, 1) - pltpu.roll(h * b, back, 1)
            e = e - al * pltpu.roll(e, step, 1) - pltpu.roll(h * e, back, 1)
            a = -al * pltpu.roll(a, step, 1)
            step *= 2
        inv = 1.0 / d
        u, v = b * inv, e * inv
        sol_u[rows, :] = u
        sol_v[rows, :] = v
        first_u[...] = jnp.where(lane == x, u[:, 0:1], first_u[...])
        first_v[...] = jnp.where(lane == x, v[:, 0:1], first_v[...])
        return 0

    first_u[...] = jnp.zeros(first_u.shape, F32)
    first_v[...] = jnp.zeros(first_v.shape, F32)
    lax.fori_loop(0, cx, depth_sweep, 0)

    pl.semaphore_wait(barrier, n_row - 1 + n_col - 1)
    exchange_row(face_s, face_r, FACE_ROWS, 0)

    await_bytes(row_bytes(face_r, FACE_ROWS), recv_sem.at[0])
    for j in range(2):
        value = strided(face_r, j)[...]
        high = value.astype(BF16).astype(F32)
        split[j] = high
        split[2 + j] = value - high
    place = strided(face_r, 2)[...]
    place_x = jnp.floor(place * (1.0 / cy))
    split[4] = place_x
    split[5] = place - place_x * cy
    slots = film.shape[1]
    x_index = lax.broadcasted_iota(jnp.int32, (cx, slots), 0).astype(F32)
    y_index = lax.broadcasted_iota(jnp.int32, (cy, slots), 0).astype(F32)

    def add_faces(pair, total):
        lefts, rights = [], []
        for half in range(2):
            src = pair * 2 + half
            in_x = x_index == split[4, pl.ds(src, 1), :]
            lefts.append(
                jnp.concatenate(
                    [jnp.where(in_x, split[j, pl.ds(src, 1), :], 0.0) for j in range(4)], axis=0
                )
            )
            rights.append(jnp.where(y_index == split[5, pl.ds(src, 1), :], 1.0, 0.0))
        left = jnp.concatenate(lefts, axis=1).astype(BF16)
        right = jnp.concatenate(rights, axis=1).astype(BF16)
        return total + lax.dot_general(
            right, left, (((1,), (1,)), ((), ())), preferred_element_type=F32
        )

    sums = lax.fori_loop(0, n_row // 2, add_faces, jnp.zeros((cy, 4 * cx), F32), unroll=True)
    wall_w = sums[:, 0:cx] + sums[:, 2 * cx : 3 * cx]
    wall_q = sums[:, cx : 2 * cx] + sums[:, 3 * cx : 4 * cx]
    alpha = (
        EXTERIOR_SHARE
        * (wall_q - wall_w * first_u[:, 0:cx])
        / (1.0 + EXTERIOR_SHARE * wall_w * first_v[:, 0:cx])
    )

    def send_k(source, target, axis, position, size, phase):
        copy = pltpu.make_async_remote_copy(
            src_ref=source,
            dst_ref=target,
            send_sem=send_sem.at[phase],
            recv_sem=recv_sem.at[phase],
            device_id={axis: lax.rem(position + size - 1, size)},
            device_id_type=MESH,
        )
        copy.start()
        return copy

    for x in range(cx):
        rows = pl.ds(x * cy, cy)
        m = mass[rows, :]
        res = props[2, rows, :]
        t = sol_u[rows, :] + alpha[:, x : x + 1] * sol_v[rows, :]
        extent = props[3, rows, :] * jnp.exp(-props[4, rows, :] / t)
        excess = (m - res) * jnp.exp(-extent)
        m2 = res + excess
        mass2[rows, :] = m2
        rhs[rows, :] = m2 * t - HEAT_OF_PYROLYSIS * (m - m2)
        cond[rows, :] = props[0, rows, :] + props[1, rows, :] * excess
        if x == 0:
            k_row_s[...] = cond[rows, :]
            k_row = send_k(k_row_s, k_row_r, "row", row, n_row, 1)
    k_col_s[...] = cond[pl.ds(0, cx, stride=cy), :]
    k_col = send_k(k_col_s, k_col_r, "col", col, n_col, 2)

    def plane(ref, x):
        return ref[pl.ds(x * cy, cy), :]

    face = (0.5 * R_X) * (plane(cond, 0) + plane(cond, 1))
    left = plane(mass2, 0) + face
    left_rhs = plane(rhs, 0)
    coupling, held, right_hand = face, face, plane(rhs, 1)
    for x in range(1, cx):
        if x < cx - 1:
            face = (0.5 * R_X) * (plane(cond, x) + plane(cond, x + 1))
        else:
            k_row.wait_recv()
            face = (0.5 * R_X) * (plane(cond, x) + k_row_r[...])
            face = jnp.where(row == n_row - 1, 0.0, face)
        inv = 1.0 / (plane(mass2, x) + held + face)
        g, l, p = face * inv, coupling * inv, right_hand * inv
        gx[x], lx[x], px[x] = g, l, p
        left = left - coupling * l
        left_rhs = left_rhs + coupling * p
        coupling = coupling * g
        held = face - face * g
        if x < cx - 1:
            right_hand = plane(rhs, x + 1) + right_hand * g
        else:
            right_hand = right_hand * g
    for j, value in enumerate((left, -coupling, held, left_rhs, right_hand)):
        strided(port_s, j)[...] = value
    exchange_row(port_s, port_r, PORT_ROWS, 3)

    k_col.wait_recv()

    def line(ref, y):
        return ref[pl.ds(y, cx, stride=cy), :]

    k_first = k_col_r[...]
    face0 = (0.5 * R_Y) * (line(cond, 0) + line(cond, 1))

    def port_y(y, carry):
        left, coupling, held, k_here = carry
        after = lax.rem(y + 1, cy)
        k_next = jnp.where(after == 0, k_first, line(cond, after))
        face = (0.5 * R_Y) * (k_here + k_next)
        face = jnp.where((after == 0) & (col == n_col - 1), 0.0, face)
        inv = 1.0 / (line(mass2, y) + held + face)
        g, l = face * inv, coupling * inv
        gy[y], dy[y], qy[y] = g, inv, l
        return left - coupling * l, coupling * g, face - face * g, k_next

    left, coupling, held, _ = lax.fori_loop(
        1, cy, port_y, (line(mass2, 0) + face0, face0, face0, line(cond, 1)), unroll=7
    )
    ypt_s[0], ypt_s[1], ypt_s[2] = left, -coupling, held
    exchange_col(ypt_s, ypt_r, 4)

    mass_out = pltpu.make_async_copy(mass2, mass_out_h, out_sem.at[0])
    mass_out.start()

    await_bytes(row_bytes(port_r, PORT_ROWS), recv_sem.at[3])
    down = strided(port_r, 1)[...]
    a = pltpu.roll(down, 1, 0)
    d = strided(port_r, 0)[...] + pltpu.roll(strided(port_r, 2)[...], 1, 0)
    b = strided(port_r, 3)[...] + pltpu.roll(strided(port_r, 4)[...], 1, 0)
    step = 1
    while step < n_row:
        inv = 1.0 / d
        h = a * inv
        back = n_row - step
        al = a * pltpu.roll(inv, step, 0)
        d = d - al * a - pltpu.roll(a * h, back, 0)
        b = b - al * pltpu.roll(b, step, 0) - pltpu.roll(h * b, back, 0)
        a = -al * pltpu.roll(a, step, 0)
        step *= 2
    first = b / d
    strided(back_s, 0)[...] = first
    strided(back_s, 1)[...] = pltpu.roll(first, n_row - 1, 0)
    exchange_row(back_s, back_r, BACK_ROWS, 5)

    def answer_y(i, carry):
        q, r = carry
        y = cy - 1 - i
        g = gy[y]
        q, r = qy[y] + g * q, g * r
        qy[y], ry[y] = q, r
        return q, r

    zero = jnp.zeros((cx, depth), F32)
    lax.fori_loop(0, cy - 1, answer_y, (zero, zero + 1.0), unroll=7)
    qy[0], ry[0] = zero + 1.0, zero

    await_bytes(ypt_r.at[pl.ds(0, n_col - 1)], recv_sem.at[4])
    diag = ypt_r[0, 0]
    for i in range(n_col):
        inv = 1.0 / diag
        yfac[0, i] = inv
        if i < n_col - 1:
            off = ypt_r[i, 1]
            yfac[1, i] = off * inv
            diag = ypt_r[i + 1, 0] + ypt_r[i, 2] - off * off * inv

    await_bytes(row_bytes(back_r, BACK_ROWS), recv_sem.at[5])
    x_first, x_next = strided(back_r, 0)[...], strided(back_r, 1)[...]
    rhs[pl.ds(0, cy), :] = x_first * plane(mass2, 0)
    for x in range(cx - 1, 0, -1):
        x_next = px[x] + gx[x] * x_next + lx[x] * x_first
        rhs[pl.ds(x * cy, cy), :] = x_next * plane(mass2, x)

    def gather_rhs(y, carry):
        value = line(rhs, y)
        return carry[0] + qy[y] * value, carry[1] + ry[y] * value

    total = lax.fori_loop(0, cy, gather_rhs, (zero, zero), unroll=8)
    yrh_s[0], yrh_s[1] = total
    exchange_col(yrh_s, yrh_r, 6)

    def forward_y(y, carry):
        carry = line(rhs, y) + gy[y - 1] * carry
        py[y] = carry
        return carry

    def backward_y(i, carry):
        y = cy - 1 - i
        carry = py[y] * dy[y] + gy[y] * carry
        py[y] = carry
        return carry

    gy[0] = zero
    lax.fori_loop(1, cy, forward_y, zero, unroll=7)
    lax.fori_loop(0, cy - 1, backward_y, zero, unroll=7)
    py[0] = zero

    await_bytes(yrh_r.at[pl.ds(0, n_col - 1)], recv_sem.at[6])
    value = yrh_r[0, 0]
    ysol[0] = value
    for i in range(1, n_col):
        value = yrh_r[i, 0] + yrh_r[i - 1, 1] - yfac[1, i - 1] * value
        ysol[i] = value
    value = value * yfac[0, n_col - 1]
    ysol[n_col - 1] = value
    ysol[n_col] = zero
    for i in range(n_col - 2, -1, -1):
        value = ysol[i] * yfac[0, i] - yfac[1, i] * value
        ysol[i] = value
    y_first, y_next = ysol[col], ysol[col + 1]

    def finish(y, _):
        out[pl.ds(y, cx, stride=cy), :] = py[y] + qy[y] * y_first + ry[y] * y_next
        return 0

    lax.fori_loop(0, cy, finish, 0, unroll=8)
    result = pltpu.make_async_copy(out, out_h, out_sem.at[1])
    result.start()

    await_bytes(row_bytes(face_s, FACE_ROWS), send_sem.at[0])
    k_row.wait_send()
    k_col.wait_send()
    await_bytes(row_bytes(port_s, PORT_ROWS), send_sem.at[3])
    await_bytes(ypt_r.at[pl.ds(0, n_col - 1)], send_sem.at[4])
    await_bytes(row_bytes(back_s, BACK_ROWS), send_sem.at[5])
    await_bytes(yrh_r.at[pl.ds(0, n_col - 1)], send_sem.at[6])
    mass_out.wait()
    result.wait()


def hand_over(a, b, a_out, b_out, sems):
    copies = [pltpu.make_async_copy(a, a_out, sems.at[0]), pltpu.make_async_copy(b, b_out, sems.at[1])]
    for copy in copies:
        copy.start()
    for copy in copies:
        copy.wait()


def per_device(n_row, n_col, kelvin, mass, labels, virgin, charred, residue, rate, energy, film, stag, elem, count):
    cx, cy, depth = kelvin.shape
    slots = film.shape[-1]
    cells = cx * cy
    vmem = lambda *shape: pltpu.VMEM(shape, F32)
    zones = virgin.shape[0]
    scratch = [
        vmem(cells, depth), vmem(cells, depth), pltpu.VMEM((cx, cy), jnp.int32),
        *[pltpu.SMEM((zones,), F32)] * 5,
        vmem(n_row, slots), vmem(n_row, slots), pltpu.VMEM((n_row, slots), jnp.int32),
        pltpu.VMEM((1, n_row), jnp.int32),
        vmem(5, cells, depth), vmem(cells, depth), vmem(cells, depth), vmem(cy, depth), vmem(cy, depth),
        vmem(n_row * 8, slots), vmem(n_row * 8, slots), vmem(6, n_row, slots),
        vmem(cells, depth), vmem(cells, depth), vmem(cells, depth),
        vmem(cy, depth), vmem(cy, depth), vmem(cx, depth), vmem(cx, depth),
        vmem(cx, cy, depth), vmem(cx, cy, depth), vmem(cx, cy, depth),
        *[vmem(n_row * 8, depth)] * 4,
        *[vmem(cy, cx, depth)] * 5,
        vmem(3, cx, depth), vmem(n_col, 3, cx, depth),
        vmem(2, cx, depth), vmem(n_col, 2, cx, depth),
        vmem(2, n_col, cx, depth), vmem(n_col + 1, cx, depth), vmem(cells, depth),
        pltpu.SemaphoreType.DMA((12,)), pltpu.SemaphoreType.DMA((2,)),
        pltpu.SemaphoreType.DMA((7,)), pltpu.SemaphoreType.DMA((7,)),
    ]
    whole = jax.ShapeDtypeStruct((cells, depth), F32)
    out, mass_out = pl.pallas_call(
        functools.partial(kernel, n_row, n_col, cx, cy, depth),
        out_shape=(whole, whole),
        in_specs=[pl.BlockSpec(memory_space=pltpu.HBM)] * 12,
        out_specs=(pl.BlockSpec(memory_space=pltpu.HBM),) * 2,
        scratch_shapes=scratch,
        compiler_params=pltpu.CompilerParams(
            collective_id=0, has_side_effects=True, vmem_limit_bytes=60 * 1024 * 1024
        ),
    )(
        kelvin.reshape(cells, depth), mass.reshape(cells, depth), labels,
        virgin, charred, residue, rate, energy,
        film.reshape(n_row, slots), stag.reshape(n_row, slots), elem.reshape(n_row, slots),
        count.reshape(1, n_row),
    )
    out, mass_out = pl.pallas_call(
        hand_over,
        out_shape=(whole, whole),
        in_specs=[pl.BlockSpec(memory_space=pltpu.HBM)] * 2,
        out_specs=(pl.BlockSpec(memory_space=pltpu.HBM),) * 2,
        scratch_shapes=[pltpu.SemaphoreType.DMA((2,))],
        compiler_params=pltpu.CompilerParams(vmem_limit_bytes=60 * 1024 * 1024),
    )(out, mass_out)
    return out.reshape(kelvin.shape), mass_out.reshape(kelvin.shape)


def solution(mesh):
    field, surface, faces = P("row", "col", None), P("row", "col"), P("row", "col", None, None)
    return jax.shard_map(
        functools.partial(per_device, mesh.shape["row"], mesh.shape["col"]),
        mesh=mesh,
        in_specs=(field, field, surface, P(), P(), P(), P(), P(), faces, faces, faces, field),
        out_specs=(field, field),
        check_vma=False,
    )
```

```python
import functools

import jax
import jax.numpy as jnp
from jax import lax
from jax.experimental import pallas as pl
from jax.experimental.pallas import tpu as pltpu
from jax.sharding import PartitionSpec as P

R_X = 32.0
R_Y = 64.0
R_Z = 1024.0
EXTERIOR_SHARE = 16.0
HEAT_OF_PYROLYSIS = 0.3

MESH = pl.DeviceIdType.MESH
F32 = jnp.float32
BF16 = jnp.bfloat16

FACE_ROWS = 4
PORT_ROWS = 5
EARLY_PLANES = 3
BACK_ROWS = 2


def kernel(
    n_row, n_col, cx, cy, depth,
    kel_h, mass_h, lab_h, virgin_h, charred_h, residue_h, rate_h, energy_h,
    film_h, stag_h, elem_h, count_h,
    py_h, qy_h, ry_h, ends_h, mass_out_h,
    kel, mass, lab, virgin_s, charred_s, residue_s, rate_s, energy_s,
    film, stag, elem, count,
    props, sol_u, sol_v, first_u, first_v,
    face_s, face_r, split, cond, mass2, rhs,
    lab_next, tops, k_col_s, k_col_r,
    gx, lx, px, port_s, port_r, back_s, back_r,
    gy, dy, qy, ry, py, ypt_s, ypt_r, yrh_s, yrh_r, yfac, ysol, ends,
    in_sem, out_sem, send_sem, recv_sem,
):
    row, col = lax.axis_index("row"), lax.axis_index("col")

    loads = [
        (film_h, film), (stag_h, stag), (elem_h, elem), (count_h, count),
        (kel_h, kel.at[pl.ds(0, cx * cy), :]), (mass_h, mass.at[pl.ds(0, cx * cy), :]), (lab_h, lab),
        (virgin_h, virgin_s), (charred_h, charred_s), (residue_h, residue_s),
        (rate_h, rate_s), (energy_h, energy_s),
    ]
    loads = [pltpu.make_async_copy(a, b, in_sem.at[i]) for i, (a, b) in enumerate(loads)]
    for load in loads:
        load.start()

    barrier = pltpu.get_barrier_semaphore()

    def row_peer(n):
        return lax.rem(row + n + 1, n_row)

    def greet_row(n, _):
        pl.semaphore_signal(barrier, inc=1, device_id={"row": row_peer(n)}, device_id_type=MESH)
        return 0

    def greet_col(t, _):
        pl.semaphore_signal(
            barrier, inc=1, device_id={"col": lax.rem(col + t, n_col)}, device_id_type=MESH
        )
        return 0

    lax.fori_loop(0, n_row - 1, greet_row, 0)
    lax.fori_loop(1, n_col, greet_col, 0)

    lane = lax.broadcasted_iota(jnp.int32, (cy, depth), 1)

    def strided(ref, value):
        return ref.at[pl.ds(value, ref.shape[0] // 8, stride=8), :]

    def slot(ref, index, rows):
        return ref.at[pl.ds(pl.multiple_of(index * 8, 8), rows), :]

    def exchange_row(source, target, rows, phase):
        def send(n, _):
            peer = row_peer(n)
            pltpu.make_async_remote_copy(
                src_ref=slot(source, peer, rows),
                dst_ref=slot(target, row, rows),
                send_sem=send_sem.at[phase],
                recv_sem=recv_sem.at[phase],
                device_id={"row": peer},
                device_id_type=MESH,
            ).start()
            return 0

        lax.fori_loop(0, n_row - 1, send, 0)
        slot(target, row, rows)[...] = slot(source, row, rows)[...]

    def row_bytes(ref, rows):
        return ref.at[pl.ds(0, (n_row - 1) * rows), :]

    def exchange_col(source, target, phase):
        def send(t, _):
            peer = lax.rem(col + t, n_col)
            pltpu.make_async_remote_copy(
                src_ref=source,
                dst_ref=target.at[col],
                send_sem=send_sem.at[phase],
                recv_sem=recv_sem.at[phase],
                device_id={"col": peer},
                device_id_type=MESH,
            ).start()
            return 0

        lax.fori_loop(1, n_col, send, 0)
        target[col] = source[...]

    def await_bytes(ref, sem):
        pltpu.make_async_copy(ref, ref, sem).wait()

    for load in loads[:4]:
        load.wait()
    counts = jnp.broadcast_to(count[...].astype(F32), (8, n_row)).T[:, 0:1]
    face_lane = lax.broadcasted_iota(jnp.int32, film.shape, 1).astype(F32)
    weight = jnp.where(face_lane < counts, film[...], 0.0)
    strided(face_s, 0)[...] = weight
    strided(face_s, 1)[...] = jnp.where(face_lane < counts, weight * stag[...], 0.0)
    place = elem[...].astype(F32)
    strided(face_s, 2)[...] = place
    place_x = jnp.floor(place * (1.0 / cy))
    split[5] = place - place_x * cy
    for j, value in enumerate((weight, weight * stag[...])):
        value = jnp.where((face_lane < counts) & (place_x == 0.0), value, 0.0)
        high = value.astype(BF16).astype(F32)
        strided(tops, j)[...] = high
        strided(tops, 2 + j)[...] = value - high
        strided(tops, 4 + j)[...] = jnp.zeros(value.shape, F32)
        strided(tops, 6 + j)[...] = jnp.zeros(value.shape, F32)
    slots = film.shape[1]
    x_index = lax.broadcasted_iota(jnp.int32, (cx, slots), 0).astype(F32)
    y_index = lax.broadcasted_iota(jnp.int32, (cy, slots), 0).astype(F32)
    contract_last = (((1,), (1,)), ((), ()))

    def add_tops(tile, _):
        right = jnp.where(y_index == split[5, pl.ds(tile, 1), :], 1.0, 0.0)
        left = tops[pl.ds(pl.multiple_of(tile * 8, 8), 8), :]
        sums = lax.dot_general(
            left.astype(BF16), right.astype(BF16), contract_last, preferred_element_type=F32
        )
        pair = [sums[j : j + 1, :] + sums[2 + j : 3 + j, :] for j in range(2)]
        if slots > 2 * cy:
            pair.append(jnp.zeros((1, slots - 2 * cy), F32))
        before = lax.rem(tile + n_row - 1, n_row)
        face_s[pl.ds(before * 8 + 3, 1), :] = jnp.concatenate(pair, axis=1)
        return 0

    lax.fori_loop(0, n_row, add_tops, 0, unroll=16)

    for load in loads[4:]:
        load.wait()

    def set_props(zone, start, planes):
        def look_up(table):
            value = jnp.full(zone.shape, table[0], F32)
            for z in range(1, 8):
                value = jnp.where(zone == z, table[z], value)
            return value

        virgin, charred, residue = look_up(virgin_s), look_up(charred_s), look_up(residue_s)
        slope = (virgin - charred) / (1.0 - residue)
        table = jnp.concatenate(
            [charred, slope, residue, look_up(rate_s), look_up(energy_s)], axis=0
        ).T
        for p in range(5):
            for x in range(planes):
                props[p, (start + x) * cy : (start + x + 1) * cy, :] = jnp.broadcast_to(
                    table[:, p * cx + x : p * cx + x + 1], (cy, depth)
                )

    set_props(lab[...], 0, cx)

    def depth_sweep(x, _):
        rows = pl.ds(pl.multiple_of(x * cy, cy), cy)
        m = mass[rows, :]
        k = props[0, rows, :] + props[1, rows, :] * (m - props[2, rows, :])
        a = jnp.where(lane == 0, 0.0, (-0.5 * R_Z) * (pltpu.roll(k, 1, 1) + k))
        d = m - a - pltpu.roll(a, depth - 1, 1)
        b = m * kel[rows, :]
        e = jnp.where(lane == 0, 1.0, 0.0)
        step = 1
        while step < depth:
            inv = 1.0 / d
            h = a * inv
            back = depth - step
            al = a * pltpu.roll(inv, step, 1)
            d = d - al * a - pltpu.roll(a * h, back, 1)
            b = b - al * pltpu.roll(b, step, 1) - pltpu.roll(h * b, back, 1)
            e = e - al * pltpu.roll(e, step, 1) - pltpu.roll(h * e, back, 1)
            a = -al * pltpu.roll(a, step, 1)
            step *= 2
        inv = 1.0 / d
        u, v = b * inv, e * inv
        sol_u[rows, :] = u
        sol_v[rows, :] = v
        first_u[...] = jnp.where(lane == x, u[:, 0:1], first_u[...])
        first_v[...] = jnp.where(lane == x, v[:, 0:1], first_v[...])
        return 0

    first_u[...] = jnp.zeros(first_u.shape, F32)
    first_v[...] = jnp.zeros(first_v.shape, F32)
    def send_before(source, target, axis, position, size, phase):
        copy = pltpu.make_async_remote_copy(
            src_ref=source,
            dst_ref=target,
            send_sem=send_sem.at[phase],
            recv_sem=recv_sem.at[phase],
            device_id={axis: lax.rem(position + size - 1, size)},
            device_id_type=MESH,
        )
        copy.start()
        return copy

    lax.fori_loop(0, EARLY_PLANES, depth_sweep, 0)
    pl.semaphore_wait(barrier, n_row - 1 + n_col - 1)
    exchange_row(face_s, face_r, FACE_ROWS, 0)
    first_rows, extra_rows = pl.ds(0, cy), pl.ds(cx * cy, cy)
    firsts = [
        send_before(kel.at[first_rows, :], kel.at[extra_rows, :], "row", row, n_row, 1),
        send_before(mass.at[first_rows, :], mass.at[extra_rows, :], "row", row, n_row, 7),
        send_before(lab, lab_next, "row", row, n_row, 8),
    ]
    lax.fori_loop(EARLY_PLANES, cx, depth_sweep, 0)
    for copy in firsts:
        copy.wait_recv()
    set_props(lab_next[...], cx, 1)
    lax.fori_loop(cx, cx + 1, depth_sweep, 0)

    await_bytes(row_bytes(face_r, FACE_ROWS), recv_sem.at[0])
    for j in range(2):
        value = strided(face_r, j)[...]
        high = value.astype(BF16).astype(F32)
        split[j] = high
        split[2 + j] = value - high
    place = strided(face_r, 2)[...]
    place_x = jnp.floor(place * (1.0 / cy))
    split[4] = place_x
    split[5] = place - place_x * cy

    def add_faces(pair, total):
        lefts, rights = [], []
        for half in range(2):
            src = pair * 2 + half
            in_x = x_index == split[4, pl.ds(src, 1), :]
            lefts.append(
                jnp.concatenate(
                    [jnp.where(in_x, split[j, pl.ds(src, 1), :], 0.0) for j in range(4)], axis=0
                )
            )
            rights.append(jnp.where(y_index == split[5, pl.ds(src, 1), :], 1.0, 0.0))
        left = jnp.concatenate(lefts, axis=1).astype(BF16)
        right = jnp.concatenate(rights, axis=1).astype(BF16)
        return total + lax.dot_general(
            right, left, contract_last, preferred_element_type=F32
        )

    sums = lax.fori_loop(0, n_row // 2, add_faces, jnp.zeros((cy, 4 * cx), F32), unroll=True)
    wall_w = sums[:, 0:cx] + sums[:, 2 * cx : 3 * cx]
    wall_q = sums[:, cx : 2 * cx] + sums[:, 3 * cx : 4 * cx]
    alpha = (
        EXTERIOR_SHARE
        * (wall_q - wall_w * first_u[:, 0:cx])
        / (1.0 + EXTERIOR_SHARE * wall_w * first_v[:, 0:cx])
    )

    next_wall = jnp.broadcast_to(jnp.sum(strided(face_r, 3)[...], axis=0, keepdims=True), (8, slots)).T
    next_w, next_q = next_wall[0:cy, 0:1], next_wall[cy : 2 * cy, 0:1]
    next_alpha = (
        EXTERIOR_SHARE
        * (next_q - next_w * first_u[:, cx : cx + 1])
        / (1.0 + EXTERIOR_SHARE * next_w * first_v[:, cx : cx + 1])
    )

    for x in range(cx + 1):
        rows = pl.ds(x * cy, cy)
        m = mass[rows, :]
        res = props[2, rows, :]
        share = alpha[:, x : x + 1] if x < cx else next_alpha
        t = sol_u[rows, :] + share * sol_v[rows, :]
        extent = props[3, rows, :] * jnp.exp(-props[4, rows, :] / t)
        excess = (m - res) * jnp.exp(-extent)
        cond[rows, :] = props[0, rows, :] + props[1, rows, :] * excess
        if x < cx:
            m2 = res + excess
            mass2[rows, :] = m2
            rhs[rows, :] = m2 * t - HEAT_OF_PYROLYSIS * (m - m2)
    k_col_s[...] = cond[pl.ds(0, cx, stride=cy), :]
    k_col = send_before(k_col_s, k_col_r, "col", col, n_col, 2)

    def plane(ref, x):
        return ref[pl.ds(x * cy, cy), :]

    face = (0.5 * R_X) * (plane(cond, 0) + plane(cond, 1))
    left = plane(mass2, 0) + face
    left_rhs = plane(rhs, 0)
    coupling, held, right_hand = face, face, plane(rhs, 1)
    for x in range(1, cx):
        face = (0.5 * R_X) * (plane(cond, x) + plane(cond, x + 1))
        if x == cx - 1:
            face = jnp.where(row == n_row - 1, 0.0, face)
        inv = 1.0 / (plane(mass2, x) + held + face)
        g, l, p = face * inv, coupling * inv, right_hand * inv
        gx[x], lx[x], px[x] = g, l, p
        left = left - coupling * l
        left_rhs = left_rhs + coupling * p
        coupling = coupling * g
        held = face - face * g
        if x < cx - 1:
            right_hand = plane(rhs, x + 1) + right_hand * g
        else:
            right_hand = right_hand * g
    for j, value in enumerate((left, -coupling, held, left_rhs, right_hand)):
        strided(port_s, j)[...] = value
    exchange_row(port_s, port_r, PORT_ROWS, 3)

    k_col.wait_recv()

    def line(ref, y):
        return ref[pl.ds(y, cx, stride=cy), :]

    k_first = k_col_r[...]
    face0 = (0.5 * R_Y) * (line(cond, 0) + line(cond, 1))

    def port_y(y, carry):
        left, coupling, held, k_here = carry
        after = lax.rem(y + 1, cy)
        k_next = jnp.where(after == 0, k_first, line(cond, after))
        face = (0.5 * R_Y) * (k_here + k_next)
        face = jnp.where((after == 0) & (col == n_col - 1), 0.0, face)
        inv = 1.0 / (line(mass2, y) + held + face)
        g, l = face * inv, coupling * inv
        gy[y], dy[y], qy[y] = g, inv, l
        return left - coupling * l, coupling * g, face - face * g, k_next

    left, coupling, held, _ = lax.fori_loop(
        1, cy, port_y, (line(mass2, 0) + face0, face0, face0, line(cond, 1)), unroll=7
    )
    ypt_s[0], ypt_s[1], ypt_s[2] = left, -coupling, held
    exchange_col(ypt_s, ypt_r, 4)

    stores = [
        pltpu.make_async_copy(a, b, out_sem.at[i])
        for i, (a, b) in enumerate(
            [(mass2, mass_out_h), (qy, qy_h), (ry, ry_h), (py, py_h), (ends, ends_h)]
        )
    ]
    stores[0].start()

    await_bytes(row_bytes(port_r, PORT_ROWS), recv_sem.at[3])
    down = strided(port_r, 1)[...]
    a = pltpu.roll(down, 1, 0)
    d = strided(port_r, 0)[...] + pltpu.roll(strided(port_r, 2)[...], 1, 0)
    b = strided(port_r, 3)[...] + pltpu.roll(strided(port_r, 4)[...], 1, 0)
    step = 1
    while step < n_row:
        inv = 1.0 / d
        h = a * inv
        back = n_row - step
        al = a * pltpu.roll(inv, step, 0)
        d = d - al * a - pltpu.roll(a * h, back, 0)
        b = b - al * pltpu.roll(b, step, 0) - pltpu.roll(h * b, back, 0)
        a = -al * pltpu.roll(a, step, 0)
        step *= 2
    first = b / d
    strided(back_s, 0)[...] = first
    strided(back_s, 1)[...] = pltpu.roll(first, n_row - 1, 0)
    exchange_row(back_s, back_r, BACK_ROWS, 5)

    def answer_y(i, carry):
        q, r = carry
        y = cy - 1 - i
        g = gy[y]
        q, r = qy[y] + g * q, g * r
        qy[y], ry[y] = q, r
        return q, r

    zero = jnp.zeros((cx, depth), F32)
    lax.fori_loop(0, cy - 1, answer_y, (zero, zero + 1.0), unroll=7)
    qy[0], ry[0] = zero + 1.0, zero
    stores[1].start()
    stores[2].start()

    await_bytes(ypt_r.at[pl.ds(0, n_col - 1)], recv_sem.at[4])
    diag = ypt_r[0, 0]
    for i in range(n_col):
        inv = 1.0 / diag
        yfac[0, i] = inv
        if i < n_col - 1:
            off = ypt_r[i, 1]
            yfac[1, i] = off * inv
            diag = ypt_r[i + 1, 0] + ypt_r[i, 2] - off * off * inv

    await_bytes(row_bytes(back_r, BACK_ROWS), recv_sem.at[5])
    x_first, x_next = strided(back_r, 0)[...], strided(back_r, 1)[...]
    rhs[pl.ds(0, cy), :] = x_first * plane(mass2, 0)
    for x in range(cx - 1, 0, -1):
        x_next = px[x] + gx[x] * x_next + lx[x] * x_first
        rhs[pl.ds(x * cy, cy), :] = x_next * plane(mass2, x)

    def gather_rhs(y, carry):
        value = line(rhs, y)
        return carry[0] + qy[y] * value, carry[1] + ry[y] * value

    total = lax.fori_loop(0, cy, gather_rhs, (zero, zero), unroll=8)
    yrh_s[0], yrh_s[1] = total
    exchange_col(yrh_s, yrh_r, 6)

    def forward_y(y, carry):
        carry = line(rhs, y) + gy[y - 1] * carry
        py[y] = carry
        return carry

    def backward_y(i, carry):
        y = cy - 1 - i
        carry = py[y] * dy[y] + gy[y] * carry
        py[y] = carry
        return carry

    gy[0] = zero
    lax.fori_loop(1, cy, forward_y, zero, unroll=7)
    lax.fori_loop(0, cy - 1, backward_y, zero, unroll=7)
    py[0] = zero
    stores[3].start()

    await_bytes(yrh_r.at[pl.ds(0, n_col - 1)], recv_sem.at[6])
    value = yrh_r[0, 0]
    ysol[0] = value
    for i in range(1, n_col):
        value = yrh_r[i, 0] + yrh_r[i - 1, 1] - yfac[1, i - 1] * value
        ysol[i] = value
    value = value * yfac[0, n_col - 1]
    ysol[n_col - 1] = value
    ysol[n_col] = zero
    for i in range(n_col - 2, -1, -1):
        value = ysol[i] * yfac[0, i] - yfac[1, i] * value
        ysol[i] = value
    ends[0], ends[1] = ysol[col], ysol[col + 1]
    stores[4].start()

    await_bytes(row_bytes(face_s, FACE_ROWS), send_sem.at[0])
    for copy in firsts:
        copy.wait_send()
    k_col.wait_send()
    await_bytes(row_bytes(port_s, PORT_ROWS), send_sem.at[3])
    await_bytes(ypt_r.at[pl.ds(0, n_col - 1)], send_sem.at[4])
    await_bytes(row_bytes(back_s, BACK_ROWS), send_sem.at[5])
    await_bytes(yrh_r.at[pl.ds(0, n_col - 1)], send_sem.at[6])
    for store in stores:
        store.wait()


def finish(cx, cy, py_h, qy_h, ry_h, ends_h, mass_h, out_h, mass_out_h, py, qy, ry, ends, mass, out, sems):
    pairs = [(ends_h, ends), (py_h, py), (qy_h, qy), (ry_h, ry), (mass_h, mass)]
    loads = [pltpu.make_async_copy(a, b, sems.at[i]) for i, (a, b) in enumerate(pairs)]
    for load in loads:
        load.start()
    for load in loads:
        load.wait()
    mass_out = pltpu.make_async_copy(mass, mass_out_h, sems.at[5])
    mass_out.start()
    first, after = ends[0], ends[1]

    def cells(y, _):
        out[pl.ds(y, cx, stride=cy), :] = py[y] + qy[y] * first + ry[y] * after
        return 0

    lax.fori_loop(0, cy, cells, 0, unroll=16)
    result = pltpu.make_async_copy(out, out_h, sems.at[6])
    result.start()
    mass_out.wait()
    result.wait()


def per_device(n_row, n_col, kelvin, mass, labels, virgin, charred, residue, rate, energy, film, stag, elem, count):
    cx, cy, depth = kelvin.shape
    slots = film.shape[-1]
    cells = cx * cy
    vmem = lambda *shape: pltpu.VMEM(shape, F32)
    zones = virgin.shape[0]
    scratch = [
        vmem(cells + cy, depth), vmem(cells + cy, depth), pltpu.VMEM((cx, cy), jnp.int32),
        *[pltpu.SMEM((zones,), F32)] * 5,
        vmem(n_row, slots), vmem(n_row, slots), pltpu.VMEM((n_row, slots), jnp.int32),
        pltpu.VMEM((1, n_row), jnp.int32),
        vmem(5, cells + cy, depth), vmem(cells + cy, depth), vmem(cells + cy, depth), vmem(cy, depth), vmem(cy, depth),
        vmem(n_row * 8, slots), vmem(n_row * 8, slots), vmem(6, n_row, slots),
        vmem(cells + cy, depth), vmem(cells, depth), vmem(cells, depth),
        pltpu.VMEM((cx, cy), jnp.int32), vmem(n_row * 8, slots), vmem(cx, depth), vmem(cx, depth),
        vmem(cx, cy, depth), vmem(cx, cy, depth), vmem(cx, cy, depth),
        *[vmem(n_row * 8, depth)] * 4,
        *[vmem(cy, cx, depth)] * 5,
        vmem(3, cx, depth), vmem(n_col, 3, cx, depth),
        vmem(2, cx, depth), vmem(n_col, 2, cx, depth),
        vmem(2, n_col, cx, depth), vmem(n_col + 1, cx, depth), vmem(2, cx, depth),
        pltpu.SemaphoreType.DMA((12,)), pltpu.SemaphoreType.DMA((5,)),
        pltpu.SemaphoreType.DMA((9,)), pltpu.SemaphoreType.DMA((9,)),
    ]
    hbm = pl.BlockSpec(memory_space=pltpu.HBM)
    whole = jax.ShapeDtypeStruct((cells, depth), F32)
    lines = jax.ShapeDtypeStruct((cy, cx, depth), F32)
    parts = pl.pallas_call(
        functools.partial(kernel, n_row, n_col, cx, cy, depth),
        out_shape=(lines, lines, lines, jax.ShapeDtypeStruct((2, cx, depth), F32), whole),
        in_specs=[hbm] * 12,
        out_specs=(hbm,) * 5,
        scratch_shapes=scratch,
        compiler_params=pltpu.CompilerParams(
            collective_id=0, has_side_effects=True, vmem_limit_bytes=60 * 1024 * 1024
        ),
    )(
        kelvin.reshape(cells, depth), mass.reshape(cells, depth), labels,
        virgin, charred, residue, rate, energy,
        film.reshape(n_row, slots), stag.reshape(n_row, slots), elem.reshape(n_row, slots),
        count.reshape(1, n_row),
    )
    out, mass_out = pl.pallas_call(
        functools.partial(finish, cx, cy),
        out_shape=(whole, whole),
        in_specs=[hbm] * 5,
        out_specs=(hbm,) * 2,
        scratch_shapes=[
            *[vmem(cy, cx, depth)] * 3, vmem(2, cx, depth), vmem(cells, depth), vmem(cells, depth),
            pltpu.SemaphoreType.DMA((7,)),
        ],
        compiler_params=pltpu.CompilerParams(vmem_limit_bytes=60 * 1024 * 1024),
    )(*parts)
    return out.reshape(kelvin.shape), mass_out.reshape(kelvin.shape)


def solution(mesh):
    field, surface, faces = P("row", "col", None), P("row", "col"), P("row", "col", None, None)
    return jax.shard_map(
        functools.partial(per_device, mesh.shape["row"], mesh.shape["col"]),
        mesh=mesh,
        in_specs=(field, field, surface, P(), P(), P(), P(), P(), faces, faces, faces, field),
        out_specs=(field, field),
        check_vma=False,
    )
```

```python
import functools

import jax
import jax.numpy as jnp
from jax import lax
from jax.experimental import pallas as pl
from jax.experimental.pallas import tpu as pltpu
from jax.sharding import PartitionSpec as P

R_X = 32.0
R_Y = 64.0
R_Z = 1024.0
EXTERIOR_SHARE = 16.0
HEAT_OF_PYROLYSIS = 0.3

MESH = pl.DeviceIdType.MESH
F32 = jnp.float32
BF16 = jnp.bfloat16

N_X = 4
FACE_ROWS = 4
PORT_ROWS = 5
EARLY_PLANES = 3
BACK_ROWS = 2


def kernel(
    n_row, n_col, cx, cy, depth,
    kel_h, mass_h, lab_h, virgin_h, charred_h, residue_h, rate_h, energy_h,
    film_h, stag_h, elem_h, count_h,
    py_h, qy_h, ry_h, ends_h, mass_out_h,
    kel, mass, lab, virgin_s, charred_s, residue_s, rate_s, energy_s,
    film, stag, elem, count,
    props, sol_u, sol_v, first_u, first_v,
    face_s, face_r, split, cond, mass2, rhs,
    lab_next, tops, k_col_s, k_col_r,
    gx, lx, px, port_s, port_r, back_s, back_r,
    gy, dy, qy, ry, py, ypt_s, ypt_r, yrh_s, yrh_r, yfac, ysol, ends,
    in_sem, out_sem, send_sem, recv_sem,
):
    row, col = lax.axis_index("row"), lax.axis_index("col")

    loads = [
        (film_h, film), (stag_h, stag), (elem_h, elem), (count_h, count),
        (kel_h, kel.at[pl.ds(0, cx * cy), :]), (mass_h, mass.at[pl.ds(0, cx * cy), :]), (lab_h, lab),
        (virgin_h, virgin_s), (charred_h, charred_s), (residue_h, residue_s),
        (rate_h, rate_s), (energy_h, energy_s),
    ]
    loads = [pltpu.make_async_copy(a, b, in_sem.at[i]) for i, (a, b) in enumerate(loads)]
    for load in loads:
        load.start()

    barrier = pltpu.get_barrier_semaphore()

    def far_first(n, size):
        return lax.rem(size + size // 2 + (n + 1) // 2 * (1 - 2 * lax.rem(n, 2)), size)

    n_z = n_row // N_X

    def row_peer(n):
        x = lax.rem(row // n_z + far_first(lax.rem(n, N_X), N_X), N_X)
        return x * n_z + lax.rem(lax.rem(row, n_z) + far_first(n // N_X, n_z), n_z)

    def greet_row(n, _):
        pl.semaphore_signal(barrier, inc=1, device_id={"row": lax.rem(row + n + 1, n_row)}, device_id_type=MESH)
        return 0

    def greet_col(t, _):
        pl.semaphore_signal(
            barrier, inc=1, device_id={"col": lax.rem(col + t, n_col)}, device_id_type=MESH
        )
        return 0

    lax.fori_loop(0, n_row - 1, greet_row, 0)
    lax.fori_loop(1, n_col, greet_col, 0)

    lane = lax.broadcasted_iota(jnp.int32, (cy, depth), 1)

    def strided(ref, value):
        return ref.at[pl.ds(value, ref.shape[0] // 8, stride=8), :]

    def slot(ref, index, rows):
        return ref.at[pl.ds(pl.multiple_of(index * 8, 8), rows), :]

    def exchange_row(source, target, rows, phase):
        def send(n, _):
            peer = row_peer(n)
            pltpu.make_async_remote_copy(
                src_ref=slot(source, peer, rows),
                dst_ref=slot(target, row, rows),
                send_sem=send_sem.at[phase],
                recv_sem=recv_sem.at[phase],
                device_id={"row": peer},
                device_id_type=MESH,
            ).start()
            return 0

        lax.fori_loop(0, n_row - 1, send, 0)
        slot(target, row, rows)[...] = slot(source, row, rows)[...]

    def row_bytes(ref, rows):
        return ref.at[pl.ds(0, (n_row - 1) * rows), :]

    def exchange_col(source, target, phase):
        def send(t, _):
            peer = lax.rem(col + t, n_col)
            pltpu.make_async_remote_copy(
                src_ref=source,
                dst_ref=target.at[col],
                send_sem=send_sem.at[phase],
                recv_sem=recv_sem.at[phase],
                device_id={"col": peer},
                device_id_type=MESH,
            ).start()
            return 0

        lax.fori_loop(1, n_col, send, 0)
        target[col] = source[...]

    def await_bytes(ref, sem):
        pltpu.make_async_copy(ref, ref, sem).wait()

    for load in loads[:4]:
        load.wait()
    counts = jnp.broadcast_to(count[...].astype(F32), (8, n_row)).T[:, 0:1]
    face_lane = lax.broadcasted_iota(jnp.int32, film.shape, 1).astype(F32)
    weight = jnp.where(face_lane < counts, film[...], 0.0)
    strided(face_s, 0)[...] = weight
    strided(face_s, 1)[...] = jnp.where(face_lane < counts, weight * stag[...], 0.0)
    place = elem[...].astype(F32)
    strided(face_s, 2)[...] = place
    place_x = jnp.floor(place * (1.0 / cy))
    split[5] = place - place_x * cy
    for j, value in enumerate((weight, weight * stag[...])):
        value = jnp.where((face_lane < counts) & (place_x == 0.0), value, 0.0)
        high = value.astype(BF16).astype(F32)
        strided(tops, j)[...] = high
        strided(tops, 2 + j)[...] = value - high
        strided(tops, 4 + j)[...] = jnp.zeros(value.shape, F32)
        strided(tops, 6 + j)[...] = jnp.zeros(value.shape, F32)
    slots = film.shape[1]
    x_index = lax.broadcasted_iota(jnp.int32, (cx, slots), 0).astype(F32)
    y_index = lax.broadcasted_iota(jnp.int32, (cy, slots), 0).astype(F32)
    contract_last = (((1,), (1,)), ((), ()))

    def add_tops(tile, _):
        right = jnp.where(y_index == split[5, pl.ds(tile, 1), :], 1.0, 0.0)
        left = tops[pl.ds(pl.multiple_of(tile * 8, 8), 8), :]
        sums = lax.dot_general(
            left.astype(BF16), right.astype(BF16), contract_last, preferred_element_type=F32
        )
        pair = [sums[j : j + 1, :] + sums[2 + j : 3 + j, :] for j in range(2)]
        if slots > 2 * cy:
            pair.append(jnp.zeros((1, slots - 2 * cy), F32))
        before = lax.rem(tile + n_row - 1, n_row)
        face_s[pl.ds(before * 8 + 3, 1), :] = jnp.concatenate(pair, axis=1)
        return 0

    lax.fori_loop(0, n_row, add_tops, 0, unroll=16)

    for load in loads[4:]:
        load.wait()

    def set_props(zone, start, planes):
        def look_up(table):
            value = jnp.full(zone.shape, table[0], F32)
            for z in range(1, 8):
                value = jnp.where(zone == z, table[z], value)
            return value

        virgin, charred, residue = look_up(virgin_s), look_up(charred_s), look_up(residue_s)
        slope = (virgin - charred) / (1.0 - residue)
        table = jnp.concatenate(
            [charred, slope, residue, look_up(rate_s), look_up(energy_s)], axis=0
        ).T
        for p in range(5):
            for x in range(planes):
                props[p, (start + x) * cy : (start + x + 1) * cy, :] = jnp.broadcast_to(
                    table[:, p * cx + x : p * cx + x + 1], (cy, depth)
                )

    set_props(lab[...], 0, cx)

    def depth_sweep(x, _):
        rows = pl.ds(pl.multiple_of(x * cy, cy), cy)
        m = mass[rows, :]
        k = props[0, rows, :] + props[1, rows, :] * (m - props[2, rows, :])
        a = jnp.where(lane == 0, 0.0, (-0.5 * R_Z) * (pltpu.roll(k, 1, 1) + k))
        d = m - a - pltpu.roll(a, depth - 1, 1)
        b = m * kel[rows, :]
        e = jnp.where(lane == 0, 1.0, 0.0)
        step = 1
        while step < depth:
            inv = 1.0 / d
            h = a * inv
            back = depth - step
            al = a * pltpu.roll(inv, step, 1)
            d = d - al * a - pltpu.roll(a * h, back, 1)
            b = b - al * pltpu.roll(b, step, 1) - pltpu.roll(h * b, back, 1)
            e = e - al * pltpu.roll(e, step, 1) - pltpu.roll(h * e, back, 1)
            a = -al * pltpu.roll(a, step, 1)
            step *= 2
        inv = 1.0 / d
        u, v = b * inv, e * inv
        sol_u[rows, :] = u
        sol_v[rows, :] = v
        first_u[...] = jnp.where(lane == x, u[:, 0:1], first_u[...])
        first_v[...] = jnp.where(lane == x, v[:, 0:1], first_v[...])
        return 0

    first_u[...] = jnp.zeros(first_u.shape, F32)
    first_v[...] = jnp.zeros(first_v.shape, F32)
    def send_before(source, target, axis, position, size, phase):
        copy = pltpu.make_async_remote_copy(
            src_ref=source,
            dst_ref=target,
            send_sem=send_sem.at[phase],
            recv_sem=recv_sem.at[phase],
            device_id={axis: lax.rem(position + size - 1, size)},
            device_id_type=MESH,
        )
        copy.start()
        return copy

    lax.fori_loop(0, EARLY_PLANES, depth_sweep, 0)
    pl.semaphore_wait(barrier, n_row - 1 + n_col - 1)
    first_rows, extra_rows = pl.ds(0, cy), pl.ds(cx * cy, cy)
    firsts = [
        send_before(kel.at[first_rows, :], kel.at[extra_rows, :], "row", row, n_row, 1),
        send_before(mass.at[first_rows, :], mass.at[extra_rows, :], "row", row, n_row, 7),
        send_before(lab, lab_next, "row", row, n_row, 8),
    ]
    exchange_row(face_s, face_r, FACE_ROWS, 0)
    lax.fori_loop(EARLY_PLANES, cx, depth_sweep, 0)
    for copy in firsts:
        copy.wait_recv()
    set_props(lab_next[...], cx, 1)
    lax.fori_loop(cx, cx + 1, depth_sweep, 0)

    await_bytes(row_bytes(face_r, FACE_ROWS), recv_sem.at[0])
    for j in range(2):
        value = strided(face_r, j)[...]
        high = value.astype(BF16).astype(F32)
        split[j] = high
        split[2 + j] = value - high
    place = strided(face_r, 2)[...]
    place_x = jnp.floor(place * (1.0 / cy))
    split[4] = place_x
    split[5] = place - place_x * cy

    def add_faces(pair, total):
        lefts, rights = [], []
        for half in range(2):
            src = pair * 2 + half
            in_x = x_index == split[4, pl.ds(src, 1), :]
            lefts.append(
                jnp.concatenate(
                    [jnp.where(in_x, split[j, pl.ds(src, 1), :], 0.0) for j in range(4)], axis=0
                )
            )
            rights.append(jnp.where(y_index == split[5, pl.ds(src, 1), :], 1.0, 0.0))
        left = jnp.concatenate(lefts, axis=1).astype(BF16)
        right = jnp.concatenate(rights, axis=1).astype(BF16)
        return total + lax.dot_general(
            right, left, contract_last, preferred_element_type=F32
        )

    sums = lax.fori_loop(0, n_row // 2, add_faces, jnp.zeros((cy, 4 * cx), F32), unroll=True)
    wall_w = sums[:, 0:cx] + sums[:, 2 * cx : 3 * cx]
    wall_q = sums[:, cx : 2 * cx] + sums[:, 3 * cx : 4 * cx]
    alpha = (
        EXTERIOR_SHARE
        * (wall_q - wall_w * first_u[:, 0:cx])
        / (1.0 + EXTERIOR_SHARE * wall_w * first_v[:, 0:cx])
    )

    next_wall = jnp.broadcast_to(jnp.sum(strided(face_r, 3)[...], axis=0, keepdims=True), (8, slots)).T
    next_w, next_q = next_wall[0:cy, 0:1], next_wall[cy : 2 * cy, 0:1]
    next_alpha = (
        EXTERIOR_SHARE
        * (next_q - next_w * first_u[:, cx : cx + 1])
        / (1.0 + EXTERIOR_SHARE * next_w * first_v[:, cx : cx + 1])
    )

    for x in range(cx + 1):
        rows = pl.ds(x * cy, cy)
        m = mass[rows, :]
        res = props[2, rows, :]
        share = alpha[:, x : x + 1] if x < cx else next_alpha
        t = sol_u[rows, :] + share * sol_v[rows, :]
        extent = props[3, rows, :] * jnp.exp(-props[4, rows, :] / t)
        excess = (m - res) * jnp.exp(-extent)
        cond[rows, :] = props[0, rows, :] + props[1, rows, :] * excess
        if x < cx:
            m2 = res + excess
            mass2[rows, :] = m2
            rhs[rows, :] = m2 * t - HEAT_OF_PYROLYSIS * (m - m2)
    k_col_s[...] = cond[pl.ds(0, cx, stride=cy), :]
    k_col = send_before(k_col_s, k_col_r, "col", col, n_col, 2)

    def plane(ref, x):
        return ref[pl.ds(x * cy, cy), :]

    face = (0.5 * R_X) * (plane(cond, 0) + plane(cond, 1))
    left = plane(mass2, 0) + face
    left_rhs = plane(rhs, 0)
    coupling, held, right_hand = face, face, plane(rhs, 1)
    for x in range(1, cx):
        face = (0.5 * R_X) * (plane(cond, x) + plane(cond, x + 1))
        if x == cx - 1:
            face = jnp.where(row == n_row - 1, 0.0, face)
        inv = 1.0 / (plane(mass2, x) + held + face)
        g, l, p = face * inv, coupling * inv, right_hand * inv
        gx[x], lx[x], px[x] = g, l, p
        left = left - coupling * l
        left_rhs = left_rhs + coupling * p
        coupling = coupling * g
        held = face - face * g
        if x < cx - 1:
            right_hand = plane(rhs, x + 1) + right_hand * g
        else:
            right_hand = right_hand * g
    for j, value in enumerate((left, -coupling, held, left_rhs, right_hand)):
        strided(port_s, j)[...] = value
    exchange_row(port_s, port_r, PORT_ROWS, 3)

    k_col.wait_recv()

    def line(ref, y):
        return ref[pl.ds(y, cx, stride=cy), :]

    k_first = k_col_r[...]
    face0 = (0.5 * R_Y) * (line(cond, 0) + line(cond, 1))

    def port_y(y, carry):
        left, coupling, held, k_here = carry
        after = lax.rem(y + 1, cy)
        k_next = jnp.where(after == 0, k_first, line(cond, after))
        face = (0.5 * R_Y) * (k_here + k_next)
        face = jnp.where((after == 0) & (col == n_col - 1), 0.0, face)
        inv = 1.0 / (line(mass2, y) + held + face)
        g, l = face * inv, coupling * inv
        gy[y], dy[y], qy[y] = g, inv, l
        return left - coupling * l, coupling * g, face - face * g, k_next

    left, coupling, held, _ = lax.fori_loop(
        1, cy, port_y, (line(mass2, 0) + face0, face0, face0, line(cond, 1)), unroll=7
    )
    ypt_s[0], ypt_s[1], ypt_s[2] = left, -coupling, held
    exchange_col(ypt_s, ypt_r, 4)

    stores = [
        pltpu.make_async_copy(a, b, out_sem.at[i])
        for i, (a, b) in enumerate(
            [(mass2, mass_out_h), (qy, qy_h), (ry, ry_h), (py, py_h), (ends, ends_h)]
        )
    ]
    stores[0].start()

    await_bytes(row_bytes(port_r, PORT_ROWS), recv_sem.at[3])
    down = strided(port_r, 1)[...]
    a = pltpu.roll(down, 1, 0)
    d = strided(port_r, 0)[...] + pltpu.roll(strided(port_r, 2)[...], 1, 0)
    b = strided(port_r, 3)[...] + pltpu.roll(strided(port_r, 4)[...], 1, 0)
    step = 1
    while step < n_row:
        inv = 1.0 / d
        h = a * inv
        back = n_row - step
        al = a * pltpu.roll(inv, step, 0)
        d = d - al * a - pltpu.roll(a * h, back, 0)
        b = b - al * pltpu.roll(b, step, 0) - pltpu.roll(h * b, back, 0)
        a = -al * pltpu.roll(a, step, 0)
        step *= 2
    first = b / d
    strided(back_s, 0)[...] = first
    strided(back_s, 1)[...] = pltpu.roll(first, n_row - 1, 0)
    exchange_row(back_s, back_r, BACK_ROWS, 5)

    def answer_y(i, carry):
        q, r = carry
        y = cy - 1 - i
        g = gy[y]
        q, r = qy[y] + g * q, g * r
        qy[y], ry[y] = q, r
        return q, r

    zero = jnp.zeros((cx, depth), F32)
    lax.fori_loop(0, cy - 1, answer_y, (zero, zero + 1.0), unroll=7)
    qy[0], ry[0] = zero + 1.0, zero
    stores[1].start()
    stores[2].start()

    await_bytes(ypt_r.at[pl.ds(0, n_col - 1)], recv_sem.at[4])
    diag = ypt_r[0, 0]
    for i in range(n_col):
        inv = 1.0 / diag
        yfac[0, i] = inv
        if i < n_col - 1:
            off = ypt_r[i, 1]
            yfac[1, i] = off * inv
            diag = ypt_r[i + 1, 0] + ypt_r[i, 2] - off * off * inv

    await_bytes(row_bytes(back_r, BACK_ROWS), recv_sem.at[5])
    x_first, x_next = strided(back_r, 0)[...], strided(back_r, 1)[...]
    rhs[pl.ds(0, cy), :] = x_first * plane(mass2, 0)
    for x in range(cx - 1, 0, -1):
        x_next = px[x] + gx[x] * x_next + lx[x] * x_first
        rhs[pl.ds(x * cy, cy), :] = x_next * plane(mass2, x)

    def gather_rhs(y, carry):
        value = line(rhs, y)
        return carry[0] + qy[y] * value, carry[1] + ry[y] * value

    total = lax.fori_loop(0, cy, gather_rhs, (zero, zero), unroll=8)
    yrh_s[0], yrh_s[1] = total
    exchange_col(yrh_s, yrh_r, 6)

    def forward_y(y, carry):
        carry = line(rhs, y) + gy[y - 1] * carry
        py[y] = carry
        return carry

    def backward_y(i, carry):
        y = cy - 1 - i
        carry = py[y] * dy[y] + gy[y] * carry
        py[y] = carry
        return carry

    gy[0] = zero
    lax.fori_loop(1, cy, forward_y, zero, unroll=7)
    lax.fori_loop(0, cy - 1, backward_y, zero, unroll=7)
    py[0] = zero
    stores[3].start()

    await_bytes(yrh_r.at[pl.ds(0, n_col - 1)], recv_sem.at[6])
    value = yrh_r[0, 0]
    ysol[0] = value
    for i in range(1, n_col):
        value = yrh_r[i, 0] + yrh_r[i - 1, 1] - yfac[1, i - 1] * value
        ysol[i] = value
    value = value * yfac[0, n_col - 1]
    ysol[n_col - 1] = value
    ysol[n_col] = zero
    for i in range(n_col - 2, -1, -1):
        value = ysol[i] * yfac[0, i] - yfac[1, i] * value
        ysol[i] = value
    ends[0], ends[1] = ysol[col], ysol[col + 1]
    stores[4].start()

    await_bytes(row_bytes(face_s, FACE_ROWS), send_sem.at[0])
    for copy in firsts:
        copy.wait_send()
    k_col.wait_send()
    await_bytes(row_bytes(port_s, PORT_ROWS), send_sem.at[3])
    await_bytes(ypt_r.at[pl.ds(0, n_col - 1)], send_sem.at[4])
    await_bytes(row_bytes(back_s, BACK_ROWS), send_sem.at[5])
    await_bytes(yrh_r.at[pl.ds(0, n_col - 1)], send_sem.at[6])
    for store in stores:
        store.wait()


def finish(cx, cy, py_h, qy_h, ry_h, ends_h, mass_h, out_h, mass_out_h, py, qy, ry, ends, mass, out, sems):
    pairs = [(ends_h, ends), (py_h, py), (qy_h, qy), (ry_h, ry), (mass_h, mass)]
    loads = [pltpu.make_async_copy(a, b, sems.at[i]) for i, (a, b) in enumerate(pairs)]
    for load in loads:
        load.start()
    for load in loads:
        load.wait()
    mass_out = pltpu.make_async_copy(mass, mass_out_h, sems.at[5])
    mass_out.start()
    first, after = ends[0], ends[1]

    def cells(y, _):
        out[pl.ds(y, cx, stride=cy), :] = py[y] + qy[y] * first + ry[y] * after
        return 0

    lax.fori_loop(0, cy, cells, 0, unroll=16)
    result = pltpu.make_async_copy(out, out_h, sems.at[6])
    result.start()
    mass_out.wait()
    result.wait()


def per_device(n_row, n_col, kelvin, mass, labels, virgin, charred, residue, rate, energy, film, stag, elem, count):
    cx, cy, depth = kelvin.shape
    slots = film.shape[-1]
    cells = cx * cy
    vmem = lambda *shape: pltpu.VMEM(shape, F32)
    zones = virgin.shape[0]
    scratch = [
        vmem(cells + cy, depth), vmem(cells + cy, depth), pltpu.VMEM((cx, cy), jnp.int32),
        *[pltpu.SMEM((zones,), F32)] * 5,
        vmem(n_row, slots), vmem(n_row, slots), pltpu.VMEM((n_row, slots), jnp.int32),
        pltpu.VMEM((1, n_row), jnp.int32),
        vmem(5, cells + cy, depth), vmem(cells + cy, depth), vmem(cells + cy, depth), vmem(cy, depth), vmem(cy, depth),
        vmem(n_row * 8, slots), vmem(n_row * 8, slots), vmem(6, n_row, slots),
        vmem(cells + cy, depth), vmem(cells, depth), vmem(cells, depth),
        pltpu.VMEM((cx, cy), jnp.int32), vmem(n_row * 8, slots), vmem(cx, depth), vmem(cx, depth),
        vmem(cx, cy, depth), vmem(cx, cy, depth), vmem(cx, cy, depth),
        *[vmem(n_row * 8, depth)] * 4,
        *[vmem(cy, cx, depth)] * 5,
        vmem(3, cx, depth), vmem(n_col, 3, cx, depth),
        vmem(2, cx, depth), vmem(n_col, 2, cx, depth),
        vmem(2, n_col, cx, depth), vmem(n_col + 1, cx, depth), vmem(2, cx, depth),
        pltpu.SemaphoreType.DMA((12,)), pltpu.SemaphoreType.DMA((5,)),
        pltpu.SemaphoreType.DMA((9,)), pltpu.SemaphoreType.DMA((9,)),
    ]
    hbm = pl.BlockSpec(memory_space=pltpu.HBM)
    whole = jax.ShapeDtypeStruct((cells, depth), F32)
    lines = jax.ShapeDtypeStruct((cy, cx, depth), F32)
    parts = pl.pallas_call(
        functools.partial(kernel, n_row, n_col, cx, cy, depth),
        out_shape=(lines, lines, lines, jax.ShapeDtypeStruct((2, cx, depth), F32), whole),
        in_specs=[hbm] * 12,
        out_specs=(hbm,) * 5,
        scratch_shapes=scratch,
        compiler_params=pltpu.CompilerParams(
            collective_id=0, has_side_effects=True, vmem_limit_bytes=60 * 1024 * 1024
        ),
    )(
        kelvin.reshape(cells, depth), mass.reshape(cells, depth), labels,
        virgin, charred, residue, rate, energy,
        film.reshape(n_row, slots), stag.reshape(n_row, slots), elem.reshape(n_row, slots),
        count.reshape(1, n_row),
    )
    out, mass_out = pl.pallas_call(
        functools.partial(finish, cx, cy),
        out_shape=(whole, whole),
        in_specs=[hbm] * 5,
        out_specs=(hbm,) * 2,
        scratch_shapes=[
            *[vmem(cy, cx, depth)] * 3, vmem(2, cx, depth), vmem(cells, depth), vmem(cells, depth),
            pltpu.SemaphoreType.DMA((7,)),
        ],
        compiler_params=pltpu.CompilerParams(vmem_limit_bytes=60 * 1024 * 1024),
    )(*parts)
    return out.reshape(kelvin.shape), mass_out.reshape(kelvin.shape)


def solution(mesh):
    field, surface, faces = P("row", "col", None), P("row", "col"), P("row", "col", None, None)
    return jax.shard_map(
        functools.partial(per_device, mesh.shape["row"], mesh.shape["col"]),
        mesh=mesh,
        in_specs=(field, field, surface, P(), P(), P(), P(), P(), faces, faces, faces, field),
        out_specs=(field, field),
        check_vma=False,
    )
```

```python
import functools

import jax
import jax.numpy as jnp
from jax import lax
from jax.experimental import pallas as pl
from jax.experimental.pallas import tpu as pltpu
from jax.sharding import PartitionSpec as P

R_X = 32.0
R_Y = 64.0
R_Z = 1024.0
EXTERIOR_SHARE = 16.0
HEAT_OF_PYROLYSIS = 0.3

MESH = pl.DeviceIdType.MESH
F32 = jnp.float32
BF16 = jnp.bfloat16

N_X = 4
FACE_ROWS = 4
PORT_ROWS = 5
EARLY_PLANES = 3
BACK_ROWS = 2


def kernel(
    n_row, n_col, cx, cy, depth,
    kel_h, mass_h, lab_h, virgin_h, charred_h, residue_h, rate_h, energy_h,
    film_h, stag_h, elem_h, count_h,
    py_h, qy_h, ry_h, ends_h, mass_out_h,
    kel, mass, lab, virgin_s, charred_s, residue_s, rate_s, energy_s,
    film, stag, elem, count,
    props, sol_u, sol_v, first_u, first_v,
    face_s, face_r, split, cond, mass2, rhs,
    lab_next, tops, k_col_s, k_col_r,
    gx, lx, px, port_s, port_r, back_s, back_r,
    gy, dy, qy, ry, py, ypt_s, ypt_r, yrh_s, yrh_r, yfac, ysol, ends,
    in_sem, out_sem, send_sem, recv_sem,
):
    row, col = lax.axis_index("row"), lax.axis_index("col")

    loads = [
        (film_h, film), (stag_h, stag), (elem_h, elem), (count_h, count),
        (kel_h, kel.at[pl.ds(0, cx * cy), :]), (mass_h, mass.at[pl.ds(0, cx * cy), :]), (lab_h, lab),
        (virgin_h, virgin_s), (charred_h, charred_s), (residue_h, residue_s),
        (rate_h, rate_s), (energy_h, energy_s),
    ]
    loads = [pltpu.make_async_copy(a, b, in_sem.at[i]) for i, (a, b) in enumerate(loads)]
    for load in loads:
        load.start()

    barrier = pltpu.get_barrier_semaphore()

    def far_first(n, size):
        return lax.rem(size + size // 2 + (n + 1) // 2 * (1 - 2 * lax.rem(n, 2)), size)

    n_z = n_row // N_X

    def row_peer(n):
        x = lax.rem(row // n_z + far_first(lax.rem(n, N_X), N_X), N_X)
        return x * n_z + lax.rem(lax.rem(row, n_z) + far_first(n // N_X, n_z), n_z)

    def greet_row(n, _):
        pl.semaphore_signal(barrier, inc=1, device_id={"row": lax.rem(row + n + 1, n_row)}, device_id_type=MESH)
        return 0

    def greet_col(t, _):
        pl.semaphore_signal(
            barrier, inc=1, device_id={"col": lax.rem(col + t, n_col)}, device_id_type=MESH
        )
        return 0

    lax.fori_loop(1, n_col, greet_col, 0)
    lax.fori_loop(0, n_row - 1, greet_row, 0)

    lane = lax.broadcasted_iota(jnp.int32, (cy, depth), 1)

    def strided(ref, value):
        return ref.at[pl.ds(value, ref.shape[0] // 8, stride=8), :]

    def slot(ref, index, rows):
        return ref.at[pl.ds(pl.multiple_of(index * 8, 8), rows), :]

    def exchange_row(source, target, rows, phase):
        def send(n, _):
            peer = row_peer(n)
            pltpu.make_async_remote_copy(
                src_ref=slot(source, peer, rows),
                dst_ref=slot(target, row, rows),
                send_sem=send_sem.at[phase],
                recv_sem=recv_sem.at[phase],
                device_id={"row": peer},
                device_id_type=MESH,
            ).start()
            return 0

        lax.fori_loop(0, n_row - 1, send, 0)
        slot(target, row, rows)[...] = slot(source, row, rows)[...]

    def row_bytes(ref, rows):
        return ref.at[pl.ds(0, (n_row - 1) * rows), :]

    def exchange_col(source, target, phase):
        def send(t, _):
            peer = lax.rem(col + t, n_col)
            pltpu.make_async_remote_copy(
                src_ref=source,
                dst_ref=target.at[col],
                send_sem=send_sem.at[phase],
                recv_sem=recv_sem.at[phase],
                device_id={"col": peer},
                device_id_type=MESH,
            ).start()
            return 0

        lax.fori_loop(1, n_col, send, 0)
        target[col] = source[...]

    def await_bytes(ref, sem):
        pltpu.make_async_copy(ref, ref, sem).wait()

    for load in loads[:4]:
        load.wait()
    counts = jnp.broadcast_to(count[...].astype(F32), (8, n_row)).T[:, 0:1]
    face_lane = lax.broadcasted_iota(jnp.int32, film.shape, 1).astype(F32)
    weight = jnp.where(face_lane < counts, film[...], 0.0)
    strided(face_s, 0)[...] = weight
    strided(face_s, 1)[...] = jnp.where(face_lane < counts, weight * stag[...], 0.0)
    place = elem[...].astype(F32)
    strided(face_s, 2)[...] = place
    place_x = jnp.floor(place * (1.0 / cy))
    split[5] = place - place_x * cy
    for j, value in enumerate((weight, weight * stag[...])):
        value = jnp.where((face_lane < counts) & (place_x == 0.0), value, 0.0)
        high = value.astype(BF16).astype(F32)
        strided(tops, j)[...] = high
        strided(tops, 2 + j)[...] = value - high
        strided(tops, 4 + j)[...] = jnp.zeros(value.shape, F32)
        strided(tops, 6 + j)[...] = jnp.zeros(value.shape, F32)
    slots = film.shape[1]
    x_index = lax.broadcasted_iota(jnp.int32, (cx, slots), 0).astype(F32)
    y_index = lax.broadcasted_iota(jnp.int32, (cy, slots), 0).astype(F32)
    contract_last = (((1,), (1,)), ((), ()))

    def add_tops(tile, _):
        right = jnp.where(y_index == split[5, pl.ds(tile, 1), :], 1.0, 0.0)
        left = tops[pl.ds(pl.multiple_of(tile * 8, 8), 8), :]
        sums = lax.dot_general(
            left.astype(BF16), right.astype(BF16), contract_last, preferred_element_type=F32
        )
        pair = [sums[j : j + 1, :] + sums[2 + j : 3 + j, :] for j in range(2)]
        if slots > 2 * cy:
            pair.append(jnp.zeros((1, slots - 2 * cy), F32))
        before = lax.rem(tile + n_row - 1, n_row)
        face_s[pl.ds(before * 8 + 3, 1), :] = jnp.concatenate(pair, axis=1)
        return 0

    lax.fori_loop(0, n_row, add_tops, 0, unroll=16)

    for load in loads[4:]:
        load.wait()

    def set_props(zone, start, planes):
        def look_up(table):
            value = jnp.full(zone.shape, table[0], F32)
            for z in range(1, 8):
                value = jnp.where(zone == z, table[z], value)
            return value

        virgin, charred, residue = look_up(virgin_s), look_up(charred_s), look_up(residue_s)
        slope = (virgin - charred) / (1.0 - residue)
        table = jnp.concatenate(
            [charred, slope, residue, look_up(rate_s), look_up(energy_s)], axis=0
        ).T
        for p in range(5):
            for x in range(planes):
                props[p, (start + x) * cy : (start + x + 1) * cy, :] = jnp.broadcast_to(
                    table[:, p * cx + x : p * cx + x + 1], (cy, depth)
                )

    set_props(lab[...], 0, cx)

    def depth_sweep(x, _):
        rows = pl.ds(pl.multiple_of(x * cy, cy), cy)
        m = mass[rows, :]
        k = props[0, rows, :] + props[1, rows, :] * (m - props[2, rows, :])
        a = jnp.where(lane == 0, 0.0, (-0.5 * R_Z) * (pltpu.roll(k, 1, 1) + k))
        d = m - a - pltpu.roll(a, depth - 1, 1)
        b = m * kel[rows, :]
        e = jnp.where(lane == 0, 1.0, 0.0)
        step = 1
        while step < depth:
            inv = 1.0 / d
            h = a * inv
            back = depth - step
            al = a * pltpu.roll(inv, step, 1)
            d = d - al * a - pltpu.roll(a * h, back, 1)
            b = b - al * pltpu.roll(b, step, 1) - pltpu.roll(h * b, back, 1)
            e = e - al * pltpu.roll(e, step, 1) - pltpu.roll(h * e, back, 1)
            a = -al * pltpu.roll(a, step, 1)
            step *= 2
        inv = 1.0 / d
        u, v = b * inv, e * inv
        sol_u[rows, :] = u
        sol_v[rows, :] = v
        first_u[...] = jnp.where(lane == x, u[:, 0:1], first_u[...])
        first_v[...] = jnp.where(lane == x, v[:, 0:1], first_v[...])
        return 0

    first_u[...] = jnp.zeros(first_u.shape, F32)
    first_v[...] = jnp.zeros(first_v.shape, F32)
    def send_before(source, target, axis, position, size, phase):
        copy = pltpu.make_async_remote_copy(
            src_ref=source,
            dst_ref=target,
            send_sem=send_sem.at[phase],
            recv_sem=recv_sem.at[phase],
            device_id={axis: lax.rem(position + size - 1, size)},
            device_id_type=MESH,
        )
        copy.start()
        return copy

    lax.fori_loop(0, EARLY_PLANES, depth_sweep, 0)
    pl.semaphore_wait(barrier, n_row - 1 + n_col - 1)
    first_rows, extra_rows = pl.ds(0, cy), pl.ds(cx * cy, cy)
    firsts = [
        send_before(kel.at[first_rows, :], kel.at[extra_rows, :], "row", row, n_row, 1),
        send_before(mass.at[first_rows, :], mass.at[extra_rows, :], "row", row, n_row, 7),
        send_before(lab, lab_next, "row", row, n_row, 8),
    ]
    exchange_row(face_s, face_r, FACE_ROWS, 0)
    lax.fori_loop(EARLY_PLANES, cx, depth_sweep, 0)
    for copy in firsts:
        copy.wait_recv()
    set_props(lab_next[...], cx, 1)
    lax.fori_loop(cx, cx + 1, depth_sweep, 0)

    await_bytes(row_bytes(face_r, FACE_ROWS), recv_sem.at[0])
    for j in range(2):
        value = strided(face_r, j)[...]
        high = value.astype(BF16).astype(F32)
        split[j] = high
        split[2 + j] = value - high
    place = strided(face_r, 2)[...]
    place_x = jnp.floor(place * (1.0 / cy))
    split[4] = place_x
    split[5] = place - place_x * cy

    def add_faces(pair, total):
        lefts, rights = [], []
        for half in range(2):
            src = pair * 2 + half
            in_x = x_index == split[4, pl.ds(src, 1), :]
            lefts.append(
                jnp.concatenate(
                    [jnp.where(in_x, split[j, pl.ds(src, 1), :], 0.0) for j in range(4)], axis=0
                )
            )
            rights.append(jnp.where(y_index == split[5, pl.ds(src, 1), :], 1.0, 0.0))
        left = jnp.concatenate(lefts, axis=1).astype(BF16)
        right = jnp.concatenate(rights, axis=1).astype(BF16)
        return total + lax.dot_general(
            right, left, contract_last, preferred_element_type=F32
        )

    sums = lax.fori_loop(0, n_row // 2, add_faces, jnp.zeros((cy, 4 * cx), F32), unroll=True)
    wall_w = sums[:, 0:cx] + sums[:, 2 * cx : 3 * cx]
    wall_q = sums[:, cx : 2 * cx] + sums[:, 3 * cx : 4 * cx]
    alpha = (
        EXTERIOR_SHARE
        * (wall_q - wall_w * first_u[:, 0:cx])
        / (1.0 + EXTERIOR_SHARE * wall_w * first_v[:, 0:cx])
    )

    next_wall = jnp.broadcast_to(jnp.sum(strided(face_r, 3)[...], axis=0, keepdims=True), (8, slots)).T
    next_w, next_q = next_wall[0:cy, 0:1], next_wall[cy : 2 * cy, 0:1]
    next_alpha = (
        EXTERIOR_SHARE
        * (next_q - next_w * first_u[:, cx : cx + 1])
        / (1.0 + EXTERIOR_SHARE * next_w * first_v[:, cx : cx + 1])
    )

    for x in range(cx + 1):
        rows = pl.ds(x * cy, cy)
        m = mass[rows, :]
        res = props[2, rows, :]
        share = alpha[:, x : x + 1] if x < cx else next_alpha
        t = sol_u[rows, :] + share * sol_v[rows, :]
        extent = props[3, rows, :] * jnp.exp(-props[4, rows, :] / t)
        excess = (m - res) * jnp.exp(-extent)
        cond[rows, :] = props[0, rows, :] + props[1, rows, :] * excess
        if x < cx:
            m2 = res + excess
            mass2[rows, :] = m2
            rhs[rows, :] = m2 * t - HEAT_OF_PYROLYSIS * (m - m2)
    k_col_s[...] = cond[pl.ds(0, cx, stride=cy), :]
    k_col = send_before(k_col_s, k_col_r, "col", col, n_col, 2)

    def plane(ref, x):
        return ref[pl.ds(x * cy, cy), :]

    face = (0.5 * R_X) * (plane(cond, 0) + plane(cond, 1))
    left = plane(mass2, 0) + face
    left_rhs = plane(rhs, 0)
    coupling, held, right_hand = face, face, plane(rhs, 1)
    for x in range(1, cx):
        face = (0.5 * R_X) * (plane(cond, x) + plane(cond, x + 1))
        if x == cx - 1:
            face = jnp.where(row == n_row - 1, 0.0, face)
        inv = 1.0 / (plane(mass2, x) + held + face)
        g, l, p = face * inv, coupling * inv, right_hand * inv
        gx[x], lx[x], px[x] = g, l, p
        left = left - coupling * l
        left_rhs = left_rhs + coupling * p
        coupling = coupling * g
        held = face - face * g
        if x < cx - 1:
            right_hand = plane(rhs, x + 1) + right_hand * g
        else:
            right_hand = right_hand * g
    for j, value in enumerate((left, -coupling, held, left_rhs, right_hand)):
        strided(port_s, j)[...] = value
    exchange_row(port_s, port_r, PORT_ROWS, 3)

    k_col.wait_recv()

    def line(ref, y):
        return ref[pl.ds(y, cx, stride=cy), :]

    k_first = k_col_r[...]
    face0 = (0.5 * R_Y) * (line(cond, 0) + line(cond, 1))

    def port_y(y, carry):
        left, coupling, held, k_here = carry
        after = lax.rem(y + 1, cy)
        k_next = jnp.where(after == 0, k_first, line(cond, after))
        face = (0.5 * R_Y) * (k_here + k_next)
        face = jnp.where((after == 0) & (col == n_col - 1), 0.0, face)
        inv = 1.0 / (line(mass2, y) + held + face)
        g, l = face * inv, coupling * inv
        gy[y], dy[y], qy[y] = g, inv, l
        return left - coupling * l, coupling * g, face - face * g, k_next

    left, coupling, held, _ = lax.fori_loop(
        1, cy, port_y, (line(mass2, 0) + face0, face0, face0, line(cond, 1)), unroll=7
    )
    ypt_s[0], ypt_s[1], ypt_s[2] = left, -coupling, held
    exchange_col(ypt_s, ypt_r, 4)

    stores = [
        pltpu.make_async_copy(a, b, out_sem.at[i])
        for i, (a, b) in enumerate(
            [(mass2, mass_out_h), (qy, qy_h), (ry, ry_h), (py, py_h), (ends, ends_h)]
        )
    ]
    stores[0].start()

    await_bytes(row_bytes(port_r, PORT_ROWS), recv_sem.at[3])
    down = strided(port_r, 1)[...]
    a = pltpu.roll(down, 1, 0)
    d = strided(port_r, 0)[...] + pltpu.roll(strided(port_r, 2)[...], 1, 0)
    b = strided(port_r, 3)[...] + pltpu.roll(strided(port_r, 4)[...], 1, 0)
    step = 1
    while step < n_row:
        inv = 1.0 / d
        h = a * inv
        back = n_row - step
        al = a * pltpu.roll(inv, step, 0)
        d = d - al * a - pltpu.roll(a * h, back, 0)
        b = b - al * pltpu.roll(b, step, 0) - pltpu.roll(h * b, back, 0)
        a = -al * pltpu.roll(a, step, 0)
        step *= 2
    first = b / d
    strided(back_s, 0)[...] = first
    strided(back_s, 1)[...] = pltpu.roll(first, n_row - 1, 0)
    exchange_row(back_s, back_r, BACK_ROWS, 5)

    def answer_y(i, carry):
        q, r = carry
        y = cy - 1 - i
        g = gy[y]
        q, r = qy[y] + g * q, g * r
        qy[y], ry[y] = q, r
        return q, r

    zero = jnp.zeros((cx, depth), F32)
    lax.fori_loop(0, cy - 1, answer_y, (zero, zero + 1.0), unroll=7)
    qy[0], ry[0] = zero + 1.0, zero
    stores[1].start()
    stores[2].start()

    await_bytes(ypt_r.at[pl.ds(0, n_col - 1)], recv_sem.at[4])
    diag = ypt_r[0, 0]
    for i in range(n_col):
        inv = 1.0 / diag
        yfac[0, i] = inv
        if i < n_col - 1:
            off = ypt_r[i, 1]
            yfac[1, i] = off * inv
            diag = ypt_r[i + 1, 0] + ypt_r[i, 2] - off * off * inv

    await_bytes(row_bytes(back_r, BACK_ROWS), recv_sem.at[5])
    x_first, x_next = strided(back_r, 0)[...], strided(back_r, 1)[...]
    rhs[pl.ds(0, cy), :] = x_first * plane(mass2, 0)
    for x in range(cx - 1, 0, -1):
        x_next = px[x] + gx[x] * x_next + lx[x] * x_first
        rhs[pl.ds(x * cy, cy), :] = x_next * plane(mass2, x)

    def gather_rhs(y, carry):
        value = line(rhs, y)
        return carry[0] + qy[y] * value, carry[1] + ry[y] * value

    total = lax.fori_loop(0, cy, gather_rhs, (zero, zero), unroll=8)
    yrh_s[0], yrh_s[1] = total
    exchange_col(yrh_s, yrh_r, 6)

    def forward_y(y, carry):
        carry = line(rhs, y) + gy[y - 1] * carry
        py[y] = carry
        return carry

    def backward_y(i, carry):
        y = cy - 1 - i
        carry = py[y] * dy[y] + gy[y] * carry
        py[y] = carry
        return carry

    gy[0] = zero
    lax.fori_loop(1, cy, forward_y, zero, unroll=7)
    lax.fori_loop(0, cy - 1, backward_y, zero, unroll=7)
    py[0] = zero
    stores[3].start()

    await_bytes(yrh_r.at[pl.ds(0, n_col - 1)], recv_sem.at[6])
    value = yrh_r[0, 0]
    ysol[0] = value
    for i in range(1, n_col):
        value = yrh_r[i, 0] + yrh_r[i - 1, 1] - yfac[1, i - 1] * value
        ysol[i] = value
    value = value * yfac[0, n_col - 1]
    ysol[n_col - 1] = value
    ysol[n_col] = zero
    for i in range(n_col - 2, -1, -1):
        value = ysol[i] * yfac[0, i] - yfac[1, i] * value
        ysol[i] = value
    ends[0], ends[1] = ysol[col], ysol[col + 1]
    stores[4].start()

    await_bytes(row_bytes(face_s, FACE_ROWS), send_sem.at[0])
    for copy in firsts:
        copy.wait_send()
    k_col.wait_send()
    await_bytes(row_bytes(port_s, PORT_ROWS), send_sem.at[3])
    await_bytes(ypt_r.at[pl.ds(0, n_col - 1)], send_sem.at[4])
    await_bytes(row_bytes(back_s, BACK_ROWS), send_sem.at[5])
    await_bytes(yrh_r.at[pl.ds(0, n_col - 1)], send_sem.at[6])
    for store in stores:
        store.wait()


def finish(cx, cy, py_h, qy_h, ry_h, ends_h, mass_h, out_h, mass_out_h, py, qy, ry, ends, mass, out, sems):
    pairs = [(ends_h, ends), (py_h, py), (qy_h, qy), (ry_h, ry), (mass_h, mass)]
    loads = [pltpu.make_async_copy(a, b, sems.at[i]) for i, (a, b) in enumerate(pairs)]
    for load in loads:
        load.start()
    for load in loads:
        load.wait()
    mass_out = pltpu.make_async_copy(mass, mass_out_h, sems.at[5])
    mass_out.start()
    first, after = ends[0], ends[1]

    def cells(y, _):
        out[pl.ds(y, cx, stride=cy), :] = py[y] + qy[y] * first + ry[y] * after
        return 0

    lax.fori_loop(0, cy, cells, 0, unroll=16)
    result = pltpu.make_async_copy(out, out_h, sems.at[6])
    result.start()
    mass_out.wait()
    result.wait()


def per_device(n_row, n_col, kelvin, mass, labels, virgin, charred, residue, rate, energy, film, stag, elem, count):
    cx, cy, depth = kelvin.shape
    slots = film.shape[-1]
    cells = cx * cy
    vmem = lambda *shape: pltpu.VMEM(shape, F32)
    zones = virgin.shape[0]
    scratch = [
        vmem(cells + cy, depth), vmem(cells + cy, depth), pltpu.VMEM((cx, cy), jnp.int32),
        *[pltpu.SMEM((zones,), F32)] * 5,
        vmem(n_row, slots), vmem(n_row, slots), pltpu.VMEM((n_row, slots), jnp.int32),
        pltpu.VMEM((1, n_row), jnp.int32),
        vmem(5, cells + cy, depth), vmem(cells + cy, depth), vmem(cells + cy, depth), vmem(cy, depth), vmem(cy, depth),
        vmem(n_row * 8, slots), vmem(n_row * 8, slots), vmem(6, n_row, slots),
        vmem(cells + cy, depth), vmem(cells, depth), vmem(cells, depth),
        pltpu.VMEM((cx, cy), jnp.int32), vmem(n_row * 8, slots), vmem(cx, depth), vmem(cx, depth),
        vmem(cx, cy, depth), vmem(cx, cy, depth), vmem(cx, cy, depth),
        *[vmem(n_row * 8, depth)] * 4,
        *[vmem(cy, cx, depth)] * 5,
        vmem(3, cx, depth), vmem(n_col, 3, cx, depth),
        vmem(2, cx, depth), vmem(n_col, 2, cx, depth),
        vmem(2, n_col, cx, depth), vmem(n_col + 1, cx, depth), vmem(2, cx, depth),
        pltpu.SemaphoreType.DMA((12,)), pltpu.SemaphoreType.DMA((5,)),
        pltpu.SemaphoreType.DMA((9,)), pltpu.SemaphoreType.DMA((9,)),
    ]
    hbm = pl.BlockSpec(memory_space=pltpu.HBM)
    whole = jax.ShapeDtypeStruct((cells, depth), F32)
    lines = jax.ShapeDtypeStruct((cy, cx, depth), F32)
    parts = pl.pallas_call(
        functools.partial(kernel, n_row, n_col, cx, cy, depth),
        out_shape=(lines, lines, lines, jax.ShapeDtypeStruct((2, cx, depth), F32), whole),
        in_specs=[hbm] * 12,
        out_specs=(hbm,) * 5,
        scratch_shapes=scratch,
        compiler_params=pltpu.CompilerParams(
            collective_id=0, has_side_effects=True, vmem_limit_bytes=60 * 1024 * 1024
        ),
    )(
        kelvin.reshape(cells, depth), mass.reshape(cells, depth), labels,
        virgin, charred, residue, rate, energy,
        film.reshape(n_row, slots), stag.reshape(n_row, slots), elem.reshape(n_row, slots),
        count.reshape(1, n_row),
    )
    out, mass_out = pl.pallas_call(
        functools.partial(finish, cx, cy),
        out_shape=(whole, whole),
        in_specs=[hbm] * 5,
        out_specs=(hbm,) * 2,
        scratch_shapes=[
            *[vmem(cy, cx, depth)] * 3, vmem(2, cx, depth), vmem(cells, depth), vmem(cells, depth),
            pltpu.SemaphoreType.DMA((7,)),
        ],
        compiler_params=pltpu.CompilerParams(vmem_limit_bytes=60 * 1024 * 1024),
    )(*parts)
    return out.reshape(kelvin.shape), mass_out.reshape(kelvin.shape)


def solution(mesh):
    field, surface, faces = P("row", "col", None), P("row", "col"), P("row", "col", None, None)
    return jax.shard_map(
        functools.partial(per_device, mesh.shape["row"], mesh.shape["col"]),
        mesh=mesh,
        in_specs=(field, field, surface, P(), P(), P(), P(), P(), faces, faces, faces, field),
        out_specs=(field, field),
        check_vma=False,
    )
```

```python
import functools

import jax
import jax.numpy as jnp
from jax import lax
from jax.experimental import pallas as pl
from jax.experimental.pallas import tpu as pltpu
from jax.sharding import PartitionSpec as P

R_X = 32.0
R_Y = 64.0
R_Z = 1024.0
EXTERIOR_SHARE = 16.0
HEAT_OF_PYROLYSIS = 0.3

MESH = pl.DeviceIdType.MESH
F32 = jnp.float32
BF16 = jnp.bfloat16

N_X = 4
FACE_ROWS = 4
PORT_ROWS = 5
EARLY_PLANES = 3
BACK_ROWS = 2


def kernel(
    n_row, n_col, cx, cy, depth,
    kel_h, mass_h, lab_h, virgin_h, charred_h, residue_h, rate_h, energy_h,
    film_h, stag_h, elem_h, count_h,
    py_h, qy_h, ry_h, ends_h, mass_out_h,
    kel, mass, lab, virgin_s, charred_s, residue_s, rate_s, energy_s,
    film, stag, elem, count,
    props, sol_u, sol_v, first_u, first_v,
    face_s, face_r, split, cond, mass2, rhs,
    lab_next, tops, k_col_s, k_col_r,
    gx, lx, px, port_s, port_r, back_s, back_r,
    gy, dy, qy, ry, py, ypt_s, ypt_r, yrh_s, yrh_r, yfac, ysol, ends,
    in_sem, out_sem, send_sem, recv_sem,
):
    row, col = lax.axis_index("row"), lax.axis_index("col")

    loads = [
        (film_h, film), (stag_h, stag), (elem_h, elem), (count_h, count),
        (kel_h, kel.at[pl.ds(0, cx * cy), :]), (mass_h, mass.at[pl.ds(0, cx * cy), :]), (lab_h, lab),
        (virgin_h, virgin_s), (charred_h, charred_s), (residue_h, residue_s),
        (rate_h, rate_s), (energy_h, energy_s),
    ]
    loads = [pltpu.make_async_copy(a, b, in_sem.at[i]) for i, (a, b) in enumerate(loads)]
    for load in loads:
        load.start()

    barrier = pltpu.get_barrier_semaphore()

    def far_first(n, size):
        return lax.rem(size + size // 2 + (n + 1) // 2 * (1 - 2 * lax.rem(n, 2)), size)

    n_z = n_row // N_X

    def row_peer(n):
        x = lax.rem(row // n_z + far_first(lax.rem(n, N_X), N_X), N_X)
        return x * n_z + lax.rem(lax.rem(row, n_z) + far_first(n // N_X, n_z), n_z)

    def greet_row(n, _):
        pl.semaphore_signal(barrier, inc=1, device_id={"row": lax.rem(row + n + 1, n_row)}, device_id_type=MESH)
        return 0

    def greet_col(t, _):
        pl.semaphore_signal(
            barrier, inc=1, device_id={"col": lax.rem(col + t, n_col)}, device_id_type=MESH
        )
        return 0

    lax.fori_loop(1, n_col, greet_col, 0)
    lax.fori_loop(0, n_row - 1, greet_row, 0)

    lane = lax.broadcasted_iota(jnp.int32, (cy, depth), 1)

    def strided(ref, value):
        return ref.at[pl.ds(value, ref.shape[0] // 8, stride=8), :]

    def slot(ref, index, rows):
        return ref.at[pl.ds(pl.multiple_of(index * 8, 8), rows), :]

    def exchange_row(source, target, rows, phase):
        def send(n, _):
            peer = row_peer(n)
            pltpu.make_async_remote_copy(
                src_ref=slot(source, peer, rows),
                dst_ref=slot(target, row, rows),
                send_sem=send_sem.at[phase],
                recv_sem=recv_sem.at[phase],
                device_id={"row": peer},
                device_id_type=MESH,
            ).start()
            return 0

        lax.fori_loop(0, n_row - 1, send, 0, unroll=True)
        slot(target, row, rows)[...] = slot(source, row, rows)[...]

    def row_bytes(ref, rows):
        return ref.at[pl.ds(0, (n_row - 1) * rows), :]

    def exchange_col(source, target, phase):
        def send(t, _):
            peer = lax.rem(col + t, n_col)
            pltpu.make_async_remote_copy(
                src_ref=source,
                dst_ref=target.at[col],
                send_sem=send_sem.at[phase],
                recv_sem=recv_sem.at[phase],
                device_id={"col": peer},
                device_id_type=MESH,
            ).start()
            return 0

        lax.fori_loop(1, n_col, send, 0)
        target[col] = source[...]

    def await_bytes(ref, sem):
        pltpu.make_async_copy(ref, ref, sem).wait()

    for load in loads[:4]:
        load.wait()
    counts = jnp.broadcast_to(count[...].astype(F32), (8, n_row)).T[:, 0:1]
    face_lane = lax.broadcasted_iota(jnp.int32, film.shape, 1).astype(F32)
    weight = jnp.where(face_lane < counts, film[...], 0.0)
    strided(face_s, 0)[...] = weight
    strided(face_s, 1)[...] = jnp.where(face_lane < counts, weight * stag[...], 0.0)
    place = elem[...].astype(F32)
    strided(face_s, 2)[...] = place
    place_x = jnp.floor(place * (1.0 / cy))
    split[5] = place - place_x * cy
    for j, value in enumerate((weight, weight * stag[...])):
        value = jnp.where((face_lane < counts) & (place_x == 0.0), value, 0.0)
        high = value.astype(BF16).astype(F32)
        strided(tops, j)[...] = high
        strided(tops, 2 + j)[...] = value - high
        strided(tops, 4 + j)[...] = jnp.zeros(value.shape, F32)
        strided(tops, 6 + j)[...] = jnp.zeros(value.shape, F32)
    slots = film.shape[1]
    x_index = lax.broadcasted_iota(jnp.int32, (cx, slots), 0).astype(F32)
    y_index = lax.broadcasted_iota(jnp.int32, (cy, slots), 0).astype(F32)
    contract_last = (((1,), (1,)), ((), ()))

    def add_tops(tile, _):
        right = jnp.where(y_index == split[5, pl.ds(tile, 1), :], 1.0, 0.0)
        left = tops[pl.ds(pl.multiple_of(tile * 8, 8), 8), :]
        sums = lax.dot_general(
            left.astype(BF16), right.astype(BF16), contract_last, preferred_element_type=F32
        )
        pair = [sums[j : j + 1, :] + sums[2 + j : 3 + j, :] for j in range(2)]
        if slots > 2 * cy:
            pair.append(jnp.zeros((1, slots - 2 * cy), F32))
        before = lax.rem(tile + n_row - 1, n_row)
        face_s[pl.ds(before * 8 + 3, 1), :] = jnp.concatenate(pair, axis=1)
        return 0

    lax.fori_loop(0, n_row, add_tops, 0, unroll=16)

    for load in loads[4:]:
        load.wait()

    def set_props(zone, start, planes):
        def look_up(table):
            value = jnp.full(zone.shape, table[0], F32)
            for z in range(1, 8):
                value = jnp.where(zone == z, table[z], value)
            return value

        virgin, charred, residue = look_up(virgin_s), look_up(charred_s), look_up(residue_s)
        slope = (virgin - charred) / (1.0 - residue)
        table = jnp.concatenate(
            [charred, slope, residue, look_up(rate_s), look_up(energy_s)], axis=0
        ).T
        for p in range(5):
            for x in range(planes):
                props[p, (start + x) * cy : (start + x + 1) * cy, :] = jnp.broadcast_to(
                    table[:, p * cx + x : p * cx + x + 1], (cy, depth)
                )

    set_props(lab[...], 0, cx)

    def depth_sweep(x, _):
        rows = pl.ds(pl.multiple_of(x * cy, cy), cy)
        m = mass[rows, :]
        k = props[0, rows, :] + props[1, rows, :] * (m - props[2, rows, :])
        a = jnp.where(lane == 0, 0.0, (-0.5 * R_Z) * (pltpu.roll(k, 1, 1) + k))
        d = m - a - pltpu.roll(a, depth - 1, 1)
        b = m * kel[rows, :]
        e = jnp.where(lane == 0, 1.0, 0.0)
        step = 1
        while step < depth:
            inv = 1.0 / d
            h = a * inv
            back = depth - step
            al = a * pltpu.roll(inv, step, 1)
            d = d - al * a - pltpu.roll(a * h, back, 1)
            b = b - al * pltpu.roll(b, step, 1) - pltpu.roll(h * b, back, 1)
            e = e - al * pltpu.roll(e, step, 1) - pltpu.roll(h * e, back, 1)
            a = -al * pltpu.roll(a, step, 1)
            step *= 2
        inv = 1.0 / d
        u, v = b * inv, e * inv
        sol_u[rows, :] = u
        sol_v[rows, :] = v
        first_u[...] = jnp.where(lane == x, u[:, 0:1], first_u[...])
        first_v[...] = jnp.where(lane == x, v[:, 0:1], first_v[...])
        return 0

    first_u[...] = jnp.zeros(first_u.shape, F32)
    first_v[...] = jnp.zeros(first_v.shape, F32)
    def send_before(source, target, axis, position, size, phase):
        copy = pltpu.make_async_remote_copy(
            src_ref=source,
            dst_ref=target,
            send_sem=send_sem.at[phase],
            recv_sem=recv_sem.at[phase],
            device_id={axis: lax.rem(position + size - 1, size)},
            device_id_type=MESH,
        )
        copy.start()
        return copy

    lax.fori_loop(0, EARLY_PLANES, depth_sweep, 0)
    pl.semaphore_wait(barrier, n_row - 1 + n_col - 1)
    first_rows, extra_rows = pl.ds(0, cy), pl.ds(cx * cy, cy)
    firsts = [
        send_before(kel.at[first_rows, :], kel.at[extra_rows, :], "row", row, n_row, 1),
        send_before(mass.at[first_rows, :], mass.at[extra_rows, :], "row", row, n_row, 7),
        send_before(lab, lab_next, "row", row, n_row, 8),
    ]
    exchange_row(face_s, face_r, FACE_ROWS, 0)
    lax.fori_loop(EARLY_PLANES, cx, depth_sweep, 0)
    for copy in firsts:
        copy.wait_recv()
    set_props(lab_next[...], cx, 1)
    lax.fori_loop(cx, cx + 1, depth_sweep, 0)

    await_bytes(row_bytes(face_r, FACE_ROWS), recv_sem.at[0])
    for j in range(2):
        value = strided(face_r, j)[...]
        high = value.astype(BF16).astype(F32)
        split[j] = high
        split[2 + j] = value - high
    place = strided(face_r, 2)[...]
    place_x = jnp.floor(place * (1.0 / cy))
    split[4] = place_x
    split[5] = place - place_x * cy

    def add_faces(pair, total):
        lefts, rights = [], []
        for half in range(2):
            src = pair * 2 + half
            in_x = x_index == split[4, pl.ds(src, 1), :]
            lefts.append(
                jnp.concatenate(
                    [jnp.where(in_x, split[j, pl.ds(src, 1), :], 0.0) for j in range(4)], axis=0
                )
            )
            rights.append(jnp.where(y_index == split[5, pl.ds(src, 1), :], 1.0, 0.0))
        left = jnp.concatenate(lefts, axis=1).astype(BF16)
        right = jnp.concatenate(rights, axis=1).astype(BF16)
        return total + lax.dot_general(
            right, left, contract_last, preferred_element_type=F32
        )

    sums = lax.fori_loop(0, n_row // 2, add_faces, jnp.zeros((cy, 4 * cx), F32), unroll=True)
    wall_w = sums[:, 0:cx] + sums[:, 2 * cx : 3 * cx]
    wall_q = sums[:, cx : 2 * cx] + sums[:, 3 * cx : 4 * cx]
    alpha = (
        EXTERIOR_SHARE
        * (wall_q - wall_w * first_u[:, 0:cx])
        / (1.0 + EXTERIOR_SHARE * wall_w * first_v[:, 0:cx])
    )

    next_wall = jnp.broadcast_to(jnp.sum(strided(face_r, 3)[...], axis=0, keepdims=True), (8, slots)).T
    next_w, next_q = next_wall[0:cy, 0:1], next_wall[cy : 2 * cy, 0:1]
    next_alpha = (
        EXTERIOR_SHARE
        * (next_q - next_w * first_u[:, cx : cx + 1])
        / (1.0 + EXTERIOR_SHARE * next_w * first_v[:, cx : cx + 1])
    )

    for x in range(cx + 1):
        rows = pl.ds(x * cy, cy)
        m = mass[rows, :]
        res = props[2, rows, :]
        share = alpha[:, x : x + 1] if x < cx else next_alpha
        t = sol_u[rows, :] + share * sol_v[rows, :]
        extent = props[3, rows, :] * jnp.exp(-props[4, rows, :] / t)
        excess = (m - res) * jnp.exp(-extent)
        cond[rows, :] = props[0, rows, :] + props[1, rows, :] * excess
        if x < cx:
            m2 = res + excess
            mass2[rows, :] = m2
            rhs[rows, :] = m2 * t - HEAT_OF_PYROLYSIS * (m - m2)
    k_col_s[...] = cond[pl.ds(0, cx, stride=cy), :]
    k_col = send_before(k_col_s, k_col_r, "col", col, n_col, 2)

    def plane(ref, x):
        return ref[pl.ds(x * cy, cy), :]

    face = (0.5 * R_X) * (plane(cond, 0) + plane(cond, 1))
    left = plane(mass2, 0) + face
    left_rhs = plane(rhs, 0)
    coupling, held, right_hand = face, face, plane(rhs, 1)
    for x in range(1, cx):
        face = (0.5 * R_X) * (plane(cond, x) + plane(cond, x + 1))
        if x == cx - 1:
            face = jnp.where(row == n_row - 1, 0.0, face)
        inv = 1.0 / (plane(mass2, x) + held + face)
        g, l, p = face * inv, coupling * inv, right_hand * inv
        gx[x], lx[x], px[x] = g, l, p
        left = left - coupling * l
        left_rhs = left_rhs + coupling * p
        coupling = coupling * g
        held = face - face * g
        if x < cx - 1:
            right_hand = plane(rhs, x + 1) + right_hand * g
        else:
            right_hand = right_hand * g
    for j, value in enumerate((left, -coupling, held, left_rhs, right_hand)):
        strided(port_s, j)[...] = value
    exchange_row(port_s, port_r, PORT_ROWS, 3)

    k_col.wait_recv()

    def line(ref, y):
        return ref[pl.ds(y, cx, stride=cy), :]

    k_first = k_col_r[...]
    face0 = (0.5 * R_Y) * (line(cond, 0) + line(cond, 1))

    def port_y(y, carry):
        left, coupling, held, k_here = carry
        after = lax.rem(y + 1, cy)
        k_next = jnp.where(after == 0, k_first, line(cond, after))
        face = (0.5 * R_Y) * (k_here + k_next)
        face = jnp.where((after == 0) & (col == n_col - 1), 0.0, face)
        inv = 1.0 / (line(mass2, y) + held + face)
        g, l = face * inv, coupling * inv
        gy[y], dy[y], qy[y] = g, inv, l
        return left - coupling * l, coupling * g, face - face * g, k_next

    left, coupling, held, _ = lax.fori_loop(
        1, cy, port_y, (line(mass2, 0) + face0, face0, face0, line(cond, 1)), unroll=7
    )
    ypt_s[0], ypt_s[1], ypt_s[2] = left, -coupling, held
    exchange_col(ypt_s, ypt_r, 4)

    stores = [
        pltpu.make_async_copy(a, b, out_sem.at[i])
        for i, (a, b) in enumerate(
            [(mass2, mass_out_h), (qy, qy_h), (ry, ry_h), (py, py_h), (ends, ends_h)]
        )
    ]
    stores[0].start()

    await_bytes(row_bytes(port_r, PORT_ROWS), recv_sem.at[3])
    down = strided(port_r, 1)[...]
    a = pltpu.roll(down, 1, 0)
    d = strided(port_r, 0)[...] + pltpu.roll(strided(port_r, 2)[...], 1, 0)
    b = strided(port_r, 3)[...] + pltpu.roll(strided(port_r, 4)[...], 1, 0)
    step = 1
    while step < n_row:
        inv = 1.0 / d
        h = a * inv
        back = n_row - step
        al = a * pltpu.roll(inv, step, 0)
        d = d - al * a - pltpu.roll(a * h, back, 0)
        b = b - al * pltpu.roll(b, step, 0) - pltpu.roll(h * b, back, 0)
        a = -al * pltpu.roll(a, step, 0)
        step *= 2
    first = b / d
    strided(back_s, 0)[...] = first
    strided(back_s, 1)[...] = pltpu.roll(first, n_row - 1, 0)
    exchange_row(back_s, back_r, BACK_ROWS, 5)

    def answer_y(i, carry):
        q, r = carry
        y = cy - 1 - i
        g = gy[y]
        q, r = qy[y] + g * q, g * r
        qy[y], ry[y] = q, r
        return q, r

    zero = jnp.zeros((cx, depth), F32)
    lax.fori_loop(0, cy - 1, answer_y, (zero, zero + 1.0), unroll=7)
    qy[0], ry[0] = zero + 1.0, zero
    stores[1].start()
    stores[2].start()

    await_bytes(ypt_r.at[pl.ds(0, n_col - 1)], recv_sem.at[4])
    diag = ypt_r[0, 0]
    for i in range(n_col):
        inv = 1.0 / diag
        yfac[0, i] = inv
        if i < n_col - 1:
            off = ypt_r[i, 1]
            yfac[1, i] = off * inv
            diag = ypt_r[i + 1, 0] + ypt_r[i, 2] - off * off * inv

    await_bytes(row_bytes(back_r, BACK_ROWS), recv_sem.at[5])
    x_first, x_next = strided(back_r, 0)[...], strided(back_r, 1)[...]
    rhs[pl.ds(0, cy), :] = x_first * plane(mass2, 0)
    for x in range(cx - 1, 0, -1):
        x_next = px[x] + gx[x] * x_next + lx[x] * x_first
        rhs[pl.ds(x * cy, cy), :] = x_next * plane(mass2, x)

    def gather_rhs(y, carry):
        value = line(rhs, y)
        return carry[0] + qy[y] * value, carry[1] + ry[y] * value

    total = lax.fori_loop(0, cy, gather_rhs, (zero, zero), unroll=8)
    yrh_s[0], yrh_s[1] = total
    exchange_col(yrh_s, yrh_r, 6)

    def forward_y(y, carry):
        carry = line(rhs, y) + gy[y - 1] * carry
        py[y] = carry
        return carry

    def backward_y(i, carry):
        y = cy - 1 - i
        carry = py[y] * dy[y] + gy[y] * carry
        py[y] = carry
        return carry

    gy[0] = zero
    lax.fori_loop(1, cy, forward_y, zero, unroll=7)
    lax.fori_loop(0, cy - 1, backward_y, zero, unroll=7)
    py[0] = zero
    stores[3].start()

    await_bytes(yrh_r.at[pl.ds(0, n_col - 1)], recv_sem.at[6])
    value = yrh_r[0, 0]
    ysol[0] = value
    for i in range(1, n_col):
        value = yrh_r[i, 0] + yrh_r[i - 1, 1] - yfac[1, i - 1] * value
        ysol[i] = value
    value = value * yfac[0, n_col - 1]
    ysol[n_col - 1] = value
    ysol[n_col] = zero
    for i in range(n_col - 2, -1, -1):
        value = ysol[i] * yfac[0, i] - yfac[1, i] * value
        ysol[i] = value
    ends[0], ends[1] = ysol[col], ysol[col + 1]
    stores[4].start()

    await_bytes(row_bytes(face_s, FACE_ROWS), send_sem.at[0])
    for copy in firsts:
        copy.wait_send()
    k_col.wait_send()
    await_bytes(row_bytes(port_s, PORT_ROWS), send_sem.at[3])
    await_bytes(ypt_r.at[pl.ds(0, n_col - 1)], send_sem.at[4])
    await_bytes(row_bytes(back_s, BACK_ROWS), send_sem.at[5])
    await_bytes(yrh_r.at[pl.ds(0, n_col - 1)], send_sem.at[6])
    for store in stores:
        store.wait()


def finish(cx, cy, py_h, qy_h, ry_h, ends_h, mass_h, out_h, mass_out_h, py, qy, ry, ends, mass, out, sems):
    pairs = [(ends_h, ends), (py_h, py), (qy_h, qy), (ry_h, ry), (mass_h, mass)]
    loads = [pltpu.make_async_copy(a, b, sems.at[i]) for i, (a, b) in enumerate(pairs)]
    for load in loads:
        load.start()
    for load in loads:
        load.wait()
    mass_out = pltpu.make_async_copy(mass, mass_out_h, sems.at[5])
    mass_out.start()
    first, after = ends[0], ends[1]

    def cells(y, _):
        out[pl.ds(y, cx, stride=cy), :] = py[y] + qy[y] * first + ry[y] * after
        return 0

    lax.fori_loop(0, cy, cells, 0, unroll=16)
    result = pltpu.make_async_copy(out, out_h, sems.at[6])
    result.start()
    mass_out.wait()
    result.wait()


def per_device(n_row, n_col, kelvin, mass, labels, virgin, charred, residue, rate, energy, film, stag, elem, count):
    cx, cy, depth = kelvin.shape
    slots = film.shape[-1]
    cells = cx * cy
    vmem = lambda *shape: pltpu.VMEM(shape, F32)
    zones = virgin.shape[0]
    scratch = [
        vmem(cells + cy, depth), vmem(cells + cy, depth), pltpu.VMEM((cx, cy), jnp.int32),
        *[pltpu.SMEM((zones,), F32)] * 5,
        vmem(n_row, slots), vmem(n_row, slots), pltpu.VMEM((n_row, slots), jnp.int32),
        pltpu.VMEM((1, n_row), jnp.int32),
        vmem(5, cells + cy, depth), vmem(cells + cy, depth), vmem(cells + cy, depth), vmem(cy, depth), vmem(cy, depth),
        vmem(n_row * 8, slots), vmem(n_row * 8, slots), vmem(6, n_row, slots),
        vmem(cells + cy, depth), vmem(cells, depth), vmem(cells, depth),
        pltpu.VMEM((cx, cy), jnp.int32), vmem(n_row * 8, slots), vmem(cx, depth), vmem(cx, depth),
        vmem(cx, cy, depth), vmem(cx, cy, depth), vmem(cx, cy, depth),
        *[vmem(n_row * 8, depth)] * 4,
        *[vmem(cy, cx, depth)] * 5,
        vmem(3, cx, depth), vmem(n_col, 3, cx, depth),
        vmem(2, cx, depth), vmem(n_col, 2, cx, depth),
        vmem(2, n_col, cx, depth), vmem(n_col + 1, cx, depth), vmem(2, cx, depth),
        pltpu.SemaphoreType.DMA((12,)), pltpu.SemaphoreType.DMA((5,)),
        pltpu.SemaphoreType.DMA((9,)), pltpu.SemaphoreType.DMA((9,)),
    ]
    hbm = pl.BlockSpec(memory_space=pltpu.HBM)
    whole = jax.ShapeDtypeStruct((cells, depth), F32)
    lines = jax.ShapeDtypeStruct((cy, cx, depth), F32)
    parts = pl.pallas_call(
        functools.partial(kernel, n_row, n_col, cx, cy, depth),
        out_shape=(lines, lines, lines, jax.ShapeDtypeStruct((2, cx, depth), F32), whole),
        in_specs=[hbm] * 12,
        out_specs=(hbm,) * 5,
        scratch_shapes=scratch,
        compiler_params=pltpu.CompilerParams(
            collective_id=0, has_side_effects=True, vmem_limit_bytes=60 * 1024 * 1024
        ),
    )(
        kelvin.reshape(cells, depth), mass.reshape(cells, depth), labels,
        virgin, charred, residue, rate, energy,
        film.reshape(n_row, slots), stag.reshape(n_row, slots), elem.reshape(n_row, slots),
        count.reshape(1, n_row),
    )
    out, mass_out = pl.pallas_call(
        functools.partial(finish, cx, cy),
        out_shape=(whole, whole),
        in_specs=[hbm] * 5,
        out_specs=(hbm,) * 2,
        scratch_shapes=[
            *[vmem(cy, cx, depth)] * 3, vmem(2, cx, depth), vmem(cells, depth), vmem(cells, depth),
            pltpu.SemaphoreType.DMA((7,)),
        ],
        compiler_params=pltpu.CompilerParams(vmem_limit_bytes=60 * 1024 * 1024),
    )(*parts)
    return out.reshape(kelvin.shape), mass_out.reshape(kelvin.shape)


def solution(mesh):
    field, surface, faces = P("row", "col", None), P("row", "col"), P("row", "col", None, None)
    return jax.shard_map(
        functools.partial(per_device, mesh.shape["row"], mesh.shape["col"]),
        mesh=mesh,
        in_specs=(field, field, surface, P(), P(), P(), P(), P(), faces, faces, faces, field),
        out_specs=(field, field),
        check_vma=False,
    )
```
